256 devices in a mesh: space: 32 (over z, x_lo, core), lib: 8 (over y, x_hi).
Axes of the slice: x: 4 (x_hi: 2, x_lo: 2; x = x_hi * 2 + x_lo), y: 4, z: 8, core: 2. Of those that a mesh axis runs over, the one named last changes fastest.
Arguments:
- targets: bfloat16 [8, 64, 131072], P(None, 'lib', 'space'), may hold values from -6 to 6
- library: bfloat16 [2560, 131072], P('lib', 'space'), may hold values from -6 to 6
- anchors: int32 [2048], P('lib'), may hold values from 7 to 295, as said below
- leads: int32 [4], replicated, may hold values from 1 to 24, as said below
- spread: float32 [64], replicated, may hold values from 0.3 to 1
Outputs:
- forecast: bfloat16 [64, 4, 131072], P('lib', None, 'space')
The draws below stay inside these ranges and needn't reach their ends.
Inputs may be any that keep to these rules, and one draw needn't show every extreme that they name: `anchors`: within each aligned block of 256 entries the positions are distinct. `leads`: Distinct.
All inputs are finite; a program needn't handle non-finite values.
Results may differ from the reference program's by a relative error of at most 0.017.
Values may be sent and summed in bfloat16 or wider, within the bound.
No kernel may reach another device: no remote copies, remote signals or barrier semaphores. Data moves between devices by JAX's collectives and lax.ppermute only.
A program may use at most 192 MiB of HBM per device.

```python
import math
import jax
import jax.numpy as jnp
from jax import lax

L = 8
LIB_DEV = 256
MAXLEAD = 24
NLEAD = 4
S = 131072
TGT = 64
BLK = 320
ANCHORS = 2048
N_LIB = 8


def draw_anchors(key, part):
    key = jax.random.fold_in(key, 11)
    lowest = L - 1
    highest = BLK - 1 - MAXLEAD
    inner = highest - lowest - 1

    def one_block(block_key):
        shuffled = jax.random.permutation(block_key, inner) + lowest + 1
        picks = jnp.concatenate([jnp.array([lowest, highest], jnp.int32), shuffled[:LIB_DEV - 2].astype(jnp.int32)])
        order = jax.random.permutation(jax.random.fold_in(block_key, 1), LIB_DEV)
        return picks[order]
    block_keys = jax.random.split(key, N_LIB)
    return jax.vmap(one_block)(block_keys).reshape(-1).astype(jnp.int32)


def draw_leads(key, part):
    key = jax.random.fold_in(key, 12)
    middle = jax.random.permutation(key, MAXLEAD - 2) + 2
    picks = jnp.concatenate([jnp.array([1, MAXLEAD], jnp.int32), middle[:NLEAD - 2].astype(jnp.int32)])
    order = jax.random.permutation(jax.random.fold_in(key, 1), NLEAD)
    return picks[order].astype(jnp.int32)


def draw_library(key, part):
    key = jax.random.fold_in(key, 13)
    shape = (BLK * N_LIB, S)
    values = jax.random.truncated_normal(key, -6.0, 6.0, shape, jnp.float32)
    return values.astype(jnp.bfloat16)


def draw_targets(key, part):
    key = jax.random.fold_in(key, 14)
    shape = (L, TGT, S)
    values = jax.random.truncated_normal(key, -6.0, 6.0, shape, jnp.float32)
    return values.astype(jnp.bfloat16)


def setup_inputs(seed: int = 0) -> dict:
    seeds = jax.random.split(jax.random.key(seed), 6)
    return {
        "targets": draw_targets(jax.random.fold_in(seeds[5], 71), 0),
        "library": draw_library(jax.random.fold_in(seeds[5], 71), 0),
        "anchors": draw_anchors(jax.random.fold_in(seeds[5], 71), 0),
        "leads": draw_leads(jax.random.fold_in(seeds[5], 71), 0),
        "spread": jnp.clip(jnp.exp(jax.random.uniform(seeds[4], (TGT,), jnp.float32, math.log(0.3), math.log(1.0))), 0.3, 1.0),
    }


def reference(targets, library, anchors, leads, spread):
    blocks = library.reshape(N_LIB, BLK, S)
    where = anchors.reshape(N_LIB, LIB_DEV).astype(jnp.int32)
    tnorm = jnp.zeros((TGT,), jnp.float32)
    for lag in range(L):
        tnorm = tnorm + lax.optimization_barrier(jnp.sum(jnp.square(targets[lag].astype(jnp.float32)), axis=1))

    def distances(carry, item):
        block, spots = item
        cross = jnp.zeros((TGT, LIB_DEV), jnp.float32)
        lnorm = jnp.zeros((LIB_DEV,), jnp.float32)
        for lag in range(L):
            rows = jnp.take(block, spots - lag, axis=0)
            cross = cross + jnp.dot(targets[lag], rows.T, preferred_element_type=jnp.float32)
            lnorm = lnorm + lax.optimization_barrier(jnp.sum(jnp.square(rows.astype(jnp.float32)), axis=1))
        return (carry, tnorm[:, None] + lnorm[None, :] - 2.0 * cross)
    _, dist = lax.scan(distances, jnp.zeros((), jnp.float32), (blocks, where))
    dist = jnp.transpose(dist, (1, 0, 2)).reshape(TGT, ANCHORS)
    scores = -dist / (spread[:, None] * math.sqrt(L * S))
    weights = jnp.exp(scores - lax.optimization_barrier(jnp.max(scores, axis=1, keepdims=True))).astype(jnp.bfloat16)
    total = lax.optimization_barrier(jnp.sum(weights.astype(jnp.float32), axis=1))
    wblocks = jnp.transpose(weights.reshape(TGT, N_LIB, LIB_DEV), (1, 0, 2))

    def compose(summed, item):
        block, spots, wpart = item
        rows = jnp.take(block, spots[None, :] + leads[:, None], axis=0)
        parts = [jnp.dot(wpart, rows[k], preferred_element_type=jnp.float32) for k in range(NLEAD)]
        part = jnp.stack(parts, axis=1).astype(jnp.bfloat16)
        return (summed + part.astype(jnp.float32), None)
    summed, _ = lax.scan(compose, jnp.zeros((TGT, NLEAD, S), jnp.float32), (blocks, where, wblocks))
    return (summed / total[:, None, None]).astype(jnp.bfloat16)
```

```python
import functools
import math

import jax
import jax.numpy as jnp
from jax import lax
from jax.experimental import pallas as pl
from jax.experimental.pallas import tpu as pltpu
from jax.sharding import Mesh, PartitionSpec as P

F32 = jnp.float32
BF16 = jnp.bfloat16
LIB = ("y", "xh")
SPACE = ("z", "xl", "co")
NEG = -3.0e38
VM = pl.BlockSpec(memory_space=pltpu.VMEM)
SM = pl.BlockSpec(memory_space=pltpu.SMEM)
PARAMS = pltpu.CompilerParams(vmem_limit_bytes=40 * 1024 * 1024)


def flip(n, bit):
    return [(i, i ^ bit) for i in range(n)]


def turn(n, by):
    return [(i, (i + by) % n) for i in range(n)]


def gather_targets(own):
    half = own.shape[0] // 2
    across = lax.ppermute(own, "xh", flip(2, 1))
    below = lax.ppermute(own, "y", turn(4, 1))
    above = lax.ppermute(own, "y", turn(4, -1))
    far_a = lax.ppermute(below[:half], "y", turn(4, 1))
    far_b = lax.ppermute(above[half:], "y", turn(4, -1))
    below_x = lax.ppermute(across, "y", turn(4, 1))
    above_x = lax.ppermute(across, "y", turn(4, -1))
    far_xa = lax.ppermute(far_a, "xh", flip(2, 1))
    far_xb = lax.ppermute(far_b, "xh", flip(2, 1))
    return (own, across, below, above, below_x, above_x, far_a, far_b, far_xa, far_xb)


def cross_kernel(lags, place, *refs):
    pieces, (block, lnorm, out, acc) = refs[:10], refs[10:]
    rows, width = block.shape
    step = 512
    acc[...] = jnp.zeros_like(acc)

    def body(i, norms):
        cols = pl.ds(pl.multiple_of(i * step, step), step)
        lhs = jnp.concatenate([p[:, cols] for p in pieces], axis=0)
        acc[:, :rows] += lax.dot_general(
            lhs, block[:, cols], (((1,), (1,)), ((), ())), preferred_element_type=F32
        )
        wide = lhs.astype(F32)
        wide = wide * wide
        part = wide[:, :128]
        for c in range(128, step, 128):
            part = part + wide[:, c : c + 128]
        return norms + part

    norms = lax.fori_loop(0, width // step, body, jnp.zeros((acc.shape[0], 128), F32))
    norms = jnp.sum(norms, axis=1, keepdims=True)
    count = acc.shape[0] // 8 // lags
    for r in range(8):
        cross = jnp.zeros((count, acc.shape[1]), F32)
        tnorm = jnp.zeros((count, 1), F32)
        for lag in range(lags):
            at = (r * lags + lag) * count
            here = acc[at : at + count, :]
            cross = cross + (pltpu.roll(here, lag, 1) if lag else here)
            tnorm = tnorm + norms[at : at + count]
        value = tnorm + lnorm[:1, :] - 2.0 * cross
        out[pl.ds(pl.multiple_of(place[r] * count, count), count), :] = value


def compose_kernel(leads, dist, mask, scale, perm, block, out):
    rows, width = block.shape
    targets = dist.shape[0]
    wide = dist.shape[1]
    scores = jnp.where(mask[:1, :] > 0.0, -dist[...] / scale[:, :1], NEG)
    top = jnp.max(scores, axis=1, keepdims=True)
    top_hi = top.astype(BF16)
    top_lo = (top - top_hi.astype(F32)).astype(BF16)
    shift = top_hi.astype(F32) + top_lo.astype(F32)
    weights = jnp.where(mask[:1, :] > 0.0, jnp.exp(scores - shift), 0.0).astype(BF16).astype(F32)
    total = jnp.sum(weights, axis=1, keepdims=True)
    tot_hi = total.astype(BF16)
    tot_lo = (total - tot_hi.astype(F32)).astype(BF16)
    count = leads.shape[0]
    stack = jnp.concatenate([pltpu.roll(weights, leads[k], 1) for k in range(count)], axis=0).astype(BF16)
    mixed = jnp.dot(perm[...], stack, preferred_element_type=F32).astype(BF16)[:, :rows]
    lane = lax.broadcasted_iota(jnp.int32, (targets, 128), 1)
    facts = jnp.where(
        lane == 0,
        top_hi.astype(F32),
        jnp.where(lane == 1, top_lo.astype(F32), jnp.where(lane == 2, tot_hi.astype(F32), tot_lo.astype(F32))),
    ).astype(BF16)
    facts = jnp.concatenate([facts] * count, axis=0)
    facts = jnp.dot(perm[...], facts, preferred_element_type=F32).astype(BF16)
    out[:, width : width + 128] = facts
    step = 512
    for c in range(0, width, step):
        out[:, c : c + step] = jnp.dot(mixed, block[:, c : c + step], preferred_element_type=F32).astype(BF16)


def combine_kernel(parts, out):
    n, rows, wide = parts.shape
    width = wide - 128
    facts = [parts[b, :, width:].astype(F32) for b in range(n)]
    tops = [f[:, 0:1] + f[:, 1:2] for f in facts]
    top = functools.reduce(jnp.maximum, tops)
    factors = [jnp.exp(t - top) for t in tops]
    total = sum(f * (x[:, 2:3] + x[:, 3:4]) for f, x in zip(factors, facts))
    factors = [f / total for f in factors]
    step = 512
    for c in range(0, width, step):
        summed = factors[0] * parts[0, :, c : c + step].astype(F32)
        for b in range(1, n):
            summed = summed + factors[b] * parts[b, :, c : c + step].astype(F32)
        out[:, c : c + step] = summed.astype(BF16)


def total_over_space(value):
    for axis, n, bit in (("co", 2, 1), ("xl", 2, 1), ("z", 8, 1), ("z", 8, 2), ("z", 8, 4)):
        value = value + lax.ppermute(value, axis, flip(n, bit))
    return value


def per_device(targets, library, anchors, leads, spread):
    lags, count, width = targets.shape
    rows = library.shape[0]
    lead_n = leads.shape[0]
    n_lib = lax.axis_size(LIB)
    n_target = count * n_lib
    wide = -(-rows // 128) * 128
    scale = math.sqrt(lags * width * lax.axis_size(SPACE))

    pieces = gather_targets(targets.reshape(lags * count, width))

    y, xh = lax.axis_index("y"), lax.axis_index("xh")
    hops = ((0, 0), (0, 1), (3, 0), (1, 0), (3, 1), (1, 1), (2, 0), (2, 1))
    place = jnp.stack([((y + dy) % 4) * 2 + (xh ^ dx) for dy, dx in hops]).astype(jnp.int32)

    norm = jnp.sum(jnp.square(library.astype(F32)), axis=1)
    norm = jnp.pad(norm, (0, wide - rows))
    lnorm = functools.reduce(jnp.add, [jnp.roll(norm, lag) for lag in range(lags)])
    lnorm = jnp.broadcast_to(lnorm[None, :], (8, wide))
    spots = lax.broadcasted_iota(jnp.int32, (wide, 1), 0)
    mask = jnp.any(spots == anchors[None, :], axis=1).astype(F32)
    mask = jnp.broadcast_to(mask[None, :], (8, wide))
    scales = jnp.broadcast_to((spread * scale)[:, None], (n_target, 128))
    row = lax.broadcasted_iota(jnp.int32, (lead_n * n_target, lead_n * n_target), 0)
    col = lax.broadcasted_iota(jnp.int32, (lead_n * n_target, lead_n * n_target), 1)
    perm = ((row % lead_n) * n_target + row // lead_n == col).astype(BF16)

    partial_dist = pl.pallas_call(
        functools.partial(cross_kernel, lags),
        out_shape=jax.ShapeDtypeStruct((n_target, wide), F32),
        in_specs=[SM] + [VM] * 12,
        out_specs=VM,
        scratch_shapes=[pltpu.VMEM((lags * n_target, wide), F32)],
        compiler_params=PARAMS,
        cost_estimate=pl.CostEstimate(flops=2 * lags * n_target * wide * width, bytes_accessed=7 << 20, transcendentals=0),
        name="cross",
    )(place, *pieces, library, lnorm)

    dist = total_over_space(partial_dist)

    parts = pl.pallas_call(
        compose_kernel,
        out_shape=jax.ShapeDtypeStruct((lead_n * n_target, width + 128), BF16),
        in_specs=[SM] + [VM] * 5,
        out_specs=VM,
        compiler_params=PARAMS,
        cost_estimate=pl.CostEstimate(flops=2 * lead_n * n_target * rows * width, bytes_accessed=5 << 20, transcendentals=n_target * wide),
        name="compose",
    )(leads, dist, mask, scales, perm, library)

    parts = parts.reshape(n_lib, lead_n * count, width + 128)
    parts = lax.all_to_all(parts, LIB, 0, 0, tiled=True)

    out = pl.pallas_call(
        combine_kernel,
        out_shape=jax.ShapeDtypeStruct((lead_n * count, width), BF16),
        in_specs=[VM],
        out_specs=VM,
        compiler_params=PARAMS,
        cost_estimate=pl.CostEstimate(flops=2 * n_target * lead_n * width, bytes_accessed=3 << 20, transcendentals=0),
        name="combine",
    )(parts)
    return out.reshape(count, lead_n, width)


def solution(mesh):
    fine = Mesh(mesh.devices.reshape(8, 2, 2, 4, 2), SPACE + LIB)
    placed = (P(None, LIB, SPACE), P(LIB, SPACE), P(LIB), P(), P())
    return jax.shard_map(per_device, mesh=fine, in_specs=placed, out_specs=P(LIB, None, SPACE), check_vma=False)
```

```python
import functools
import math

import jax
import jax.numpy as jnp
from jax import lax
from jax.experimental import pallas as pl
from jax.experimental.pallas import tpu as pltpu
from jax.sharding import Mesh, PartitionSpec as P

F32 = jnp.float32
BF16 = jnp.bfloat16
LIB = ("y", "xh")
SPACE = ("z", "xl", "co")
FAR = 3.0e38
VM = pl.BlockSpec(memory_space=pltpu.VMEM)
SM = pl.BlockSpec(memory_space=pltpu.SMEM)
PARAMS = pltpu.CompilerParams(vmem_limit_bytes=16 * 1024 * 1024)
NEAR = ((0, 0), (0, 1), (3, 0), (1, 0))
AWAY = ((3, 1), (1, 1), (2, 0), (2, 1))


def flip(n, bit):
    return [(i, i ^ bit) for i in range(n)]


def turn(n, by):
    return [(i, (i + by) % n) for i in range(n)]


def gather_targets(own):
    half = own.shape[0] // 2
    across = lax.ppermute(own, "xh", flip(2, 1))
    below = lax.ppermute(own, "y", turn(4, 1))
    above = lax.ppermute(own, "y", turn(4, -1))
    far_a = lax.ppermute(below[:half], "y", turn(4, 1))
    far_b = lax.ppermute(above[half:], "y", turn(4, -1))
    below_x = lax.ppermute(across, "y", turn(4, 1))
    above_x = lax.ppermute(across, "y", turn(4, -1))
    far_xa = lax.ppermute(far_a, "xh", flip(2, 1))
    far_xb = lax.ppermute(far_b, "xh", flip(2, 1))
    return (own, across, below, above), (below_x, above_x, far_a, far_b, far_xa, far_xb)


def cross_rows(lags, pieces, block, lnorm, acc):
    rows, width = block.shape
    step = 512
    acc[...] = jnp.zeros_like(acc)

    def body(i, norms):
        cols = pl.ds(pl.multiple_of(i * step, step), step)
        lhs = jnp.concatenate([p[:, cols] for p in pieces], axis=0)
        acc[:, :rows] += lax.dot_general(
            lhs, block[:, cols], (((1,), (1,)), ((), ())), preferred_element_type=F32
        )
        wide = lhs.astype(F32)
        wide = wide * wide
        part = wide[:, :128]
        for c in range(128, step, 128):
            part = part + wide[:, c : c + 128]
        return norms + part

    norms = lax.fori_loop(0, width // step, body, jnp.zeros((acc.shape[0], 128), F32))
    norms = jnp.sum(norms, axis=1, keepdims=True)
    count = acc.shape[0] // 4 // lags
    values = []
    for r in range(4):
        cross = jnp.zeros((count, acc.shape[1]), F32)
        tnorm = jnp.zeros((count, 1), F32)
        for lag in range(lags):
            at = (r * lags + lag) * count
            here = acc[at : at + count, :]
            cross = cross + (pltpu.roll(here, lag, 1) if lag else here)
            tnorm = tnorm + norms[at : at + count]
        values.append(tnorm + lnorm[:1, :] - 2.0 * cross)
    return values


def near_kernel(lags, *refs):
    pieces, (block, lnorm, out, acc) = refs[:4], refs[4:]
    out[...] = jnp.concatenate(cross_rows(lags, pieces, block, lnorm, acc), axis=0)


def away_kernel(lags, place, *refs):
    pieces, (block, lnorm, near, out, acc) = refs[:6], refs[6:]
    values = cross_rows(lags, pieces, block, lnorm, acc)
    count = values[0].shape[0]
    for r, (dy, dx) in enumerate(NEAR + AWAY):
        owner = lax.rem(place[0] + dy, 4) * 2 + lax.rem(place[1] + dx, 2)
        value = near[r * count : (r + 1) * count, :] if r < 4 else values[r - 4]
        out[pl.ds(pl.multiple_of(owner * count, count), count), :] = value


def compose_kernel(leads, dist, dist_other, scale, perm, block, block_other, out):
    rows, width = block.shape
    targets = dist.shape[0]
    both = [-d[...] / scale[:, :1] for d in (dist, dist_other)]
    top = functools.reduce(jnp.maximum, [jnp.max(s, axis=1, keepdims=True) for s in both])
    top_hi = top.astype(BF16)
    top_lo = (top - top_hi.astype(F32)).astype(BF16)
    shift = top_hi.astype(F32) + top_lo.astype(F32)
    both = [jnp.exp(s - shift).astype(BF16).astype(F32) for s in both]
    total = sum(jnp.sum(w, axis=1, keepdims=True) for w in both)
    tot_hi = total.astype(BF16)
    tot_lo = (total - tot_hi.astype(F32)).astype(BF16)
    count = leads.shape[0]
    mixed = []
    for weights in both:
        stack = jnp.concatenate([pltpu.roll(weights, leads[k], 1) for k in range(count)], axis=0).astype(BF16)
        mixed.append(jnp.dot(perm[...], stack, preferred_element_type=F32).astype(BF16)[:, :rows])
    lane = lax.broadcasted_iota(jnp.int32, (targets, 128), 1)
    facts = jnp.where(
        lane == 0,
        top_hi.astype(F32),
        jnp.where(lane == 1, top_lo.astype(F32), jnp.where(lane == 2, tot_hi.astype(F32), tot_lo.astype(F32))),
    ).astype(BF16)
    facts = jnp.concatenate([facts] * count, axis=0)
    facts = jnp.dot(perm[...], facts, preferred_element_type=F32).astype(BF16)
    out[:, width : width + 128] = facts
    step = 512
    for c in range(0, width, step):
        value = jnp.dot(mixed[0], block[:, c : c + step], preferred_element_type=F32)
        value = value + jnp.dot(mixed[1], block_other[:, c : c + step], preferred_element_type=F32)
        out[:, c : c + step] = value.astype(BF16)


def combine_kernel(parts, out):
    n, rows, wide = parts.shape
    width = wide - 128
    count, lead_n, _ = out.shape
    facts = [parts[b, :, width:].astype(F32) for b in range(n)]
    tops = [f[:, 0:1] + f[:, 1:2] for f in facts]
    top = functools.reduce(jnp.maximum, tops)
    factors = [jnp.exp(t - top) for t in tops]
    total = 0.5 * sum(f * (x[:, 2:3] + x[:, 3:4]) for f, x in zip(factors, facts))
    factors = [f / total for f in factors]
    step = 512
    for h in range(2):
        mine = [b for b in range(n) if (b // 2) % 2 == h]
        for c in range(0, width, step):
            summed = sum(factors[b] * parts[b, :, c : c + step].astype(F32) for b in mine)
            summed = summed.reshape(count, lead_n, step).astype(BF16)
            out[:, :, h * width + c : h * width + c + step] = summed


def total_over_space(value):
    value = value + lax.ppermute(value, "co", flip(2, 1))
    value = value + lax.ppermute(value, "xl", flip(2, 1))
    down = lax.ppermute(value, "z", turn(8, 1))
    up = lax.ppermute(value, "z", turn(8, -1))
    three, two = value + down + up, value + up
    high = lax.ppermute(three, "z", turn(8, -3))
    low = lax.ppermute(two, "z", turn(8, 3))
    return three + high + low


def per_device(targets, library, anchors, leads, spread):
    lags, count, width = targets.shape
    rows = library.shape[0]
    lead_n = leads.shape[0]
    n_lib = lax.axis_size(LIB)
    n_target = count * n_lib
    wide = -(-rows // 128) * 128
    scale = math.sqrt(lags * width * lax.axis_size(SPACE))
    half = width // 2

    near, away = gather_targets(targets.reshape(lags * count, width))

    y, xh = lax.axis_index("y"), lax.axis_index("xh")
    place = jnp.stack([y, xh]).astype(jnp.int32)
    norm = jnp.sum(jnp.square(library.astype(F32)), axis=1)
    norm = jnp.pad(norm, (0, wide - rows))
    lnorm = functools.reduce(jnp.add, [jnp.roll(norm, lag) for lag in range(lags)])
    lnorm = jnp.broadcast_to(lnorm[None, :], (8, wide))
    spots = lax.broadcasted_iota(jnp.int32, (wide, 1), 0)
    chosen = jnp.any(spots == anchors[None, :], axis=1)
    scales = jnp.broadcast_to((spread * scale)[:, None], (n_target, 128))
    row = lax.broadcasted_iota(jnp.int32, (lead_n * n_target, lead_n * n_target), 0)
    col = lax.broadcasted_iota(jnp.int32, (lead_n * n_target, lead_n * n_target), 1)
    perm = ((row % lead_n) * n_target + row // lead_n == col).astype(BF16)

    flops = lags * n_target * wide * width
    near_dist = pl.pallas_call(
        functools.partial(near_kernel, lags),
        out_shape=jax.ShapeDtypeStruct((n_target // 2, wide), F32),
        in_specs=[VM] * 6,
        out_specs=VM,
        scratch_shapes=[pltpu.VMEM((lags * n_target // 2, wide), F32)],
        compiler_params=PARAMS,
        cost_estimate=pl.CostEstimate(flops=flops, bytes_accessed=5 << 20, transcendentals=0),
        name="near",
    )(*near, library, lnorm)
    partial_dist = pl.pallas_call(
        functools.partial(away_kernel, lags),
        out_shape=jax.ShapeDtypeStruct((n_target, wide), F32),
        in_specs=[SM] + [VM] * 9,
        out_specs=VM,
        scratch_shapes=[pltpu.VMEM((lags * n_target // 2, wide), F32)],
        compiler_params=PARAMS,
        cost_estimate=pl.CostEstimate(flops=flops, bytes_accessed=5 << 20, transcendentals=0),
        name="away",
    )(place, *away, library, lnorm, near_dist)

    mine = lax.rem(y, 2) * half
    kept = lax.dynamic_slice_in_dim(library, mine, half, axis=1)
    given = lax.dynamic_slice_in_dim(library, half - mine, half, axis=1)
    given, partial_dist = lax.optimization_barrier((given, partial_dist))
    other = lax.ppermute(given, "y", flip(4, 1))

    dist = total_over_space(partial_dist)
    dist = jnp.where(chosen[None, :], dist, FAR)
    dist_other = lax.ppermute(dist, "y", flip(4, 1))

    parts = pl.pallas_call(
        compose_kernel,
        out_shape=jax.ShapeDtypeStruct((lead_n * n_target, half + 128), BF16),
        in_specs=[SM] + [VM] * 6,
        out_specs=VM,
        compiler_params=PARAMS,
        cost_estimate=pl.CostEstimate(flops=2 * lead_n * n_target * rows * width, bytes_accessed=5 << 20, transcendentals=n_target * wide),
        name="compose",
    )(leads, dist, dist_other, scales, perm, kept, other)

    parts = parts.reshape(n_lib, lead_n * count, half + 128)
    parts = lax.all_to_all(parts, LIB, 0, 0, tiled=True)

    return pl.pallas_call(
        combine_kernel,
        out_shape=jax.ShapeDtypeStruct((count, lead_n, width), BF16),
        in_specs=[VM],
        out_specs=VM,
        compiler_params=PARAMS,
        cost_estimate=pl.CostEstimate(flops=2 * n_target * lead_n * width, bytes_accessed=3 << 20, transcendentals=0),
        name="combine",
    )(parts)


def solution(mesh):
    fine = Mesh(mesh.devices.reshape(8, 2, 2, 4, 2), SPACE + LIB)
    placed = (P(None, LIB, SPACE), P(LIB, SPACE), P(LIB), P(), P())
    return jax.shard_map(per_device, mesh=fine, in_specs=placed, out_specs=P(LIB, None, SPACE), check_vma=False)
```

```python
import functools
import math

import jax
import jax.numpy as jnp
from jax import lax
from jax.experimental import pallas as pl
from jax.experimental.pallas import tpu as pltpu
from jax.sharding import Mesh, PartitionSpec as P

F32 = jnp.float32
BF16 = jnp.bfloat16
Y = ("yh", "yl")
LIB = ("yh", "yl", "xh")
SPACE = ("z", "xl", "co")
CHIPS = ("xl", "co")
VM = pl.BlockSpec(memory_space=pltpu.VMEM)
SM = pl.BlockSpec(memory_space=pltpu.SMEM)
PARAMS = pltpu.CompilerParams(vmem_limit_bytes=16 * 1024 * 1024)
NEAR = ((0, 0), (0, 1), (3, 0), (1, 0))
AWAY = ((3, 1), (1, 1), (2, 0), (2, 1))


def flip(n, bit):
    return [(i, i ^ bit) for i in range(n)]


def turn(n, by):
    return [(i, (i + by) % n) for i in range(n)]


def gather_targets(own):
    half = own.shape[0] // 2
    across = lax.ppermute(own, "xh", flip(2, 1))
    below = lax.ppermute(own, Y, turn(4, 1))
    above = lax.ppermute(own, Y, turn(4, -1))
    far_a = lax.ppermute(below[:half], Y, turn(4, 1))
    far_b = lax.ppermute(above[half:], Y, turn(4, -1))
    below_x = lax.ppermute(across, Y, turn(4, 1))
    above_x = lax.ppermute(across, Y, turn(4, -1))
    far_xa = lax.ppermute(far_a, "xh", flip(2, 1))
    far_xb = lax.ppermute(far_b, "xh", flip(2, 1))
    return (own, across, below, above), (below_x, above_x, far_a, far_b, far_xa, far_xb)


def cross_rows(lags, pieces, block, lnorm, acc):
    rows, width = block.shape
    acc[...] = jnp.zeros_like(acc)
    lhs = jnp.concatenate([p[...] for p in pieces], axis=0)
    acc[:, :rows] = lax.dot_general(lhs, block[...], (((1,), (1,)), ((), ())), preferred_element_type=F32)
    norms = jnp.zeros((acc.shape[0], 128), F32)
    for c in range(0, width, 128):
        part = lhs[:, c : c + 128].astype(F32)
        norms = norms + part * part
    norms = jnp.sum(norms, axis=1, keepdims=True)
    count = acc.shape[0] // 4 // lags
    values = []
    for r in range(4):
        cross = jnp.zeros((count, acc.shape[1]), F32)
        tnorm = jnp.zeros((count, 1), F32)
        for lag in range(lags):
            at = (r * lags + lag) * count
            here = acc[at : at + count, :]
            cross = cross + (pltpu.roll(here, lag, 1) if lag else here)
            tnorm = tnorm + norms[at : at + count]
        values.append(tnorm + lnorm[:1, :] - 2.0 * cross)
    return values


def near_kernel(lags, *refs):
    pieces, (block, lnorm, out, acc) = refs[:4], refs[4:]
    out[...] = jnp.concatenate(cross_rows(lags, pieces, block, lnorm, acc), axis=0)


def away_kernel(lags, place, *refs):
    pieces, (block, lnorm, near, picks, out, acc) = refs[:6], refs[6:]
    values = cross_rows(lags, pieces, block, lnorm, acc)
    count = values[0].shape[0]
    value = jnp.concatenate([near[...]] + values, axis=0)
    first = value.astype(BF16)
    rest = value - first.astype(F32)
    second = rest.astype(BF16)
    third = (rest - second.astype(F32)).astype(BF16)
    picked = [jnp.dot(part, picks[...], preferred_element_type=F32) for part in (first, second, third)]
    value = picked[0] + picked[1] + picked[2]
    for r, (dy, dx) in enumerate(NEAR + AWAY):
        owner = lax.rem(place[0] + dy, 4) * 2 + lax.rem(place[1] + dx, 2)
        out[pl.ds(pl.multiple_of(owner * count, count), count), :] = value[r * count : (r + 1) * count, :]


def weights_kernel(dist, scale, spots, out):
    summed = dist[0]
    for i in range(1, dist.shape[0]):
        summed = summed + dist[i]
    scores = -summed / scale[:, :1]
    top = jnp.max(scores, axis=1, keepdims=True)
    top_hi = top.astype(BF16)
    top_lo = (top - top_hi.astype(F32)).astype(BF16)
    shift = top_hi.astype(F32) + top_lo.astype(F32)
    weights = jnp.exp(scores - shift).astype(BF16)
    weights = jnp.dot(weights, spots[...], preferred_element_type=F32).astype(BF16)
    lane = lax.broadcasted_iota(jnp.int32, (weights.shape[0], 128), 1)
    facts = jnp.where(lane == 0, top_hi.astype(F32), top_lo.astype(F32)).astype(BF16)
    weights = jnp.concatenate([weights, facts], axis=1)
    for i in range(out.shape[0]):
        out[i] = weights


def compose_kernel(leads, place, given, perm, block, block_other, out):
    rows, width = block.shape
    sides = given.shape[0] // 2
    mine = lax.rem(place[0], 2)
    both = [
        jnp.concatenate([given[2 * i + at].astype(F32) for i in range(sides)], axis=0) for at in (mine, 1 - mine)
    ]
    wide = both[0].shape[1] - 128
    tops = [w[:, wide : wide + 1] + w[:, wide + 1 : wide + 2] for w in both]
    larger = tops[0] >= tops[1]
    top = jnp.where(larger, tops[0], tops[1])
    top_hi = jnp.where(larger, both[0][:, wide : wide + 1], both[1][:, wide : wide + 1])
    top_lo = jnp.where(larger, both[0][:, wide + 1 : wide + 2], both[1][:, wide + 1 : wide + 2])
    both = [(w[:, :wide] * jnp.exp(t - top)).astype(BF16).astype(F32) for w, t in zip(both, tops)]
    total = jnp.sum(both[0] + both[1], axis=1, keepdims=True)
    tot_hi = total.astype(BF16).astype(F32)
    tot_lo = total - tot_hi
    count = leads.shape[0]
    mixed = []
    for weights in both:
        stack = jnp.concatenate([pltpu.roll(weights, leads[k], 1) for k in range(count)], axis=0).astype(BF16)
        mixed.append(jnp.dot(perm[...], stack, preferred_element_type=F32).astype(BF16)[:, :rows])
    lane = lax.broadcasted_iota(jnp.int32, (total.shape[0], 128), 1)
    facts = jnp.where(lane == 0, top_hi, jnp.where(lane == 1, top_lo, jnp.where(lane == 2, tot_hi, tot_lo)))
    facts = jnp.concatenate([facts.astype(BF16)] * count, axis=0)
    facts = jnp.dot(perm[...], facts, preferred_element_type=F32).astype(BF16)
    out[:, width : width + 128] = facts
    step = 512
    for c in range(0, width, step):
        value = jnp.dot(mixed[0], block[:, c : c + step], preferred_element_type=F32)
        value = value + jnp.dot(mixed[1], block_other[:, c : c + step], preferred_element_type=F32)
        out[:, c : c + step] = value.astype(BF16)


def combine_kernel(parts, out):
    n, rows, wide = parts.shape
    width = wide - 128
    count, lead_n, _ = out.shape
    facts = [parts[b, :, width:].astype(F32) for b in range(n)]
    tops = [f[:, 0:1] + f[:, 1:2] for f in facts]
    top = functools.reduce(jnp.maximum, tops)
    factors = [jnp.exp(t - top) for t in tops]
    total = 0.5 * sum(f * (x[:, 2:3] + x[:, 3:4]) for f, x in zip(factors, facts))
    factors = [f / total for f in factors]
    step = 512
    for h in range(2):
        mine = [b for b in range(n) if (b // 2) % 2 == h]
        for c in range(0, width, step):
            summed = sum(factors[b] * parts[b, :, c : c + step].astype(F32) for b in mine)
            summed = summed.reshape(count, lead_n, step).astype(BF16)
            out[:, :, h * width + c : h * width + c + step] = summed


def per_device(targets, library, anchors, leads, spread):
    lags, count, width = targets.shape
    rows = library.shape[0]
    lead_n = leads.shape[0]
    n_lib = lax.axis_size(LIB)
    n_target = count * n_lib
    wide = -(-rows // 128) * 128
    scale = math.sqrt(lags * width * lax.axis_size(SPACE))
    half = width // 2

    near, away = gather_targets(targets.reshape(lags * count, width))

    y, xh = lax.axis_index(Y), lax.axis_index("xh")
    place = jnp.stack([y, xh]).astype(jnp.int32)
    norm = jnp.sum(jnp.square(library.astype(F32)), axis=1)
    norm = jnp.pad(norm, (0, wide - rows))
    lnorm = functools.reduce(jnp.add, [jnp.roll(norm, lag) for lag in range(lags)])
    lnorm = jnp.broadcast_to(lnorm[None, :], (8, wide))
    spots = lax.broadcasted_iota(jnp.int32, (anchors.shape[0], wide), 1)
    spots = (spots == anchors[:, None]).astype(BF16)
    picks = lax.broadcasted_iota(jnp.int32, (wide, anchors.shape[0]), 0)
    picks = (picks == anchors[None, :]).astype(BF16)
    group = lax.axis_size(CHIPS)
    few = n_target // group
    scales = lax.dynamic_slice_in_dim(spread, lax.axis_index(CHIPS) * few, few) * scale
    scales = jnp.broadcast_to(scales[:, None], (few, 128))
    row = lax.broadcasted_iota(jnp.int32, (lead_n * n_target, lead_n * n_target), 0)
    col = lax.broadcasted_iota(jnp.int32, (lead_n * n_target, lead_n * n_target), 1)
    perm = ((row % lead_n) * n_target + row // lead_n == col).astype(BF16)

    flops = lags * n_target * wide * width
    near_dist = pl.pallas_call(
        functools.partial(near_kernel, lags),
        out_shape=jax.ShapeDtypeStruct((n_target // 2, wide), F32),
        in_specs=[VM] * 6,
        out_specs=VM,
        scratch_shapes=[pltpu.VMEM((lags * n_target // 2, wide), F32)],
        compiler_params=PARAMS,
        cost_estimate=pl.CostEstimate(flops=flops, bytes_accessed=5 << 20, transcendentals=0),
        name="near",
    )(*near, library, lnorm)
    partial_dist = pl.pallas_call(
        functools.partial(away_kernel, lags),
        out_shape=jax.ShapeDtypeStruct((n_target, anchors.shape[0]), F32),
        in_specs=[SM] + [VM] * 10,
        out_specs=VM,
        scratch_shapes=[pltpu.VMEM((lags * n_target // 2, wide), F32)],
        compiler_params=PARAMS,
        cost_estimate=pl.CostEstimate(flops=flops, bytes_accessed=5 << 20, transcendentals=0),
        name="away",
    )(place, *away, library, lnorm, near_dist, picks)

    mine = lax.rem(y, 2) * half
    kept = lax.dynamic_slice_in_dim(library, mine, half, axis=1)
    given = lax.dynamic_slice_in_dim(library, half - mine, half, axis=1)
    given, partial_dist = lax.optimization_barrier((given, partial_dist))
    other = lax.ppermute(given, Y, flip(4, 1))

    dist = partial_dist.reshape(group, few, anchors.shape[0])
    dist = jnp.sum(lax.all_to_all(dist, CHIPS, 0, 0, tiled=True), axis=0)
    dist = jnp.broadcast_to(dist[None], (lax.axis_size("z"),) + dist.shape)
    dist = lax.all_to_all(dist, "z", 0, 0, tiled=True)

    weights = pl.pallas_call(
        weights_kernel,
        out_shape=jax.ShapeDtypeStruct((2 * group, few, wide + 128), BF16),
        in_specs=[VM] * 3,
        out_specs=VM,
        compiler_params=PARAMS,
        cost_estimate=pl.CostEstimate(flops=2 * few * wide * 256, bytes_accessed=1 << 20, transcendentals=few * 256),
        name="weights",
    )(dist, scales, spots)
    weights = lax.all_to_all(weights, CHIPS + ("yl",), 0, 0, tiled=True)

    parts = pl.pallas_call(
        compose_kernel,
        out_shape=jax.ShapeDtypeStruct((lead_n * n_target, half + 128), BF16),
        in_specs=[SM] * 2 + [VM] * 4,
        out_specs=VM,
        compiler_params=PARAMS,
        cost_estimate=pl.CostEstimate(flops=2 * lead_n * n_target * rows * width, bytes_accessed=5 << 20, transcendentals=n_target * wide),
        name="compose",
    )(leads, place, weights, perm, kept, other)

    parts = parts.reshape(n_lib, lead_n * count, half + 128)
    parts = lax.all_to_all(parts, LIB, 0, 0, tiled=True)

    return pl.pallas_call(
        combine_kernel,
        out_shape=jax.ShapeDtypeStruct((count, lead_n, width), BF16),
        in_specs=[VM],
        out_specs=VM,
        compiler_params=PARAMS,
        cost_estimate=pl.CostEstimate(flops=2 * n_target * lead_n * width, bytes_accessed=3 << 20, transcendentals=0),
        name="combine",
    )(parts)


def solution(mesh):
    fine = Mesh(mesh.devices.reshape(8, 2, 2, 2, 2, 2), SPACE + LIB)
    placed = (P(None, LIB, SPACE), P(LIB, SPACE), P(LIB), P(), P())
    return jax.shard_map(per_device, mesh=fine, in_specs=placed, out_specs=P(LIB, None, SPACE), check_vma=False)
```

```python
import functools
import math

import jax
import jax.numpy as jnp
from jax import lax
from jax.experimental import pallas as pl
from jax.experimental.pallas import tpu as pltpu
from jax.sharding import Mesh, PartitionSpec as P

F32 = jnp.float32
BF16 = jnp.bfloat16
Y = ("yh", "yl")
LIB = ("yh", "yl", "xh")
SPACE = ("z", "xl", "co")
VM = pl.BlockSpec(memory_space=pltpu.VMEM)
SM = pl.BlockSpec(memory_space=pltpu.SMEM)
PARAMS = pltpu.CompilerParams(vmem_limit_bytes=16 * 1024 * 1024)
NEAR = ((0, 0), (0, 1), (3, 0), (1, 0))
AWAY = ((3, 1), (1, 1), (2, 0), (2, 1))


def flip(n, bit):
    return [(i, i ^ bit) for i in range(n)]


def turn(n, by):
    return [(i, (i + by) % n) for i in range(n)]


def gather_targets(own):
    half = own.shape[0] // 2
    across = lax.ppermute(own, "xh", flip(2, 1))
    below = lax.ppermute(own, Y, turn(4, 1))
    above = lax.ppermute(own, Y, turn(4, -1))
    far_a = lax.ppermute(below[:half], Y, turn(4, 1))
    far_b = lax.ppermute(above[half:], Y, turn(4, -1))
    below_x = lax.ppermute(across, Y, turn(4, 1))
    above_x = lax.ppermute(across, Y, turn(4, -1))
    far_xa = lax.ppermute(far_a, "xh", flip(2, 1))
    far_xb = lax.ppermute(far_b, "xh", flip(2, 1))
    return (own, across, below, above), (below_x, above_x, far_a, far_b, far_xa, far_xb)


def cross_rows(lags, pieces, block, lnorm, acc):
    rows, width = block.shape
    acc[...] = jnp.zeros_like(acc)
    lhs = jnp.concatenate([p[...] for p in pieces], axis=0)
    acc[:, :rows] = lax.dot_general(lhs, block[...], (((1,), (1,)), ((), ())), preferred_element_type=F32)
    norms = jnp.zeros((acc.shape[0], 128), F32)
    for c in range(0, width, 128):
        part = lhs[:, c : c + 128].astype(F32)
        norms = norms + part * part
    norms = jnp.sum(norms, axis=1, keepdims=True)
    count = acc.shape[0] // 4 // lags
    values = []
    for r in range(4):
        cross = jnp.zeros((count, acc.shape[1]), F32)
        tnorm = jnp.zeros((count, 1), F32)
        for lag in range(lags):
            at = (r * lags + lag) * count
            here = acc[at : at + count, :]
            cross = cross + (pltpu.roll(here, lag, 1) if lag else here)
            tnorm = tnorm + norms[at : at + count]
        values.append(tnorm + lnorm[:1, :] - 2.0 * cross)
    return values


def near_kernel(lags, *refs):
    pieces, (block, lnorm, out, acc) = refs[:4], refs[4:]
    out[...] = jnp.concatenate(cross_rows(lags, pieces, block, lnorm, acc), axis=0)


def away_kernel(lags, place, *refs):
    pieces, (block, lnorm, near, picks, out, acc) = refs[:6], refs[6:]
    values = cross_rows(lags, pieces, block, lnorm, acc)
    count = values[0].shape[0]
    value = jnp.concatenate([near[...]] + values, axis=0)
    first = value.astype(BF16)
    rest = value - first.astype(F32)
    second = rest.astype(BF16)
    third = (rest - second.astype(F32)).astype(BF16)
    picked = [jnp.dot(part, picks[...], preferred_element_type=F32) for part in (first, second, third)]
    value = picked[0] + picked[1] + picked[2]
    for r, (dy, dx) in enumerate(NEAR + AWAY):
        owner = lax.rem(place[0] + dy, 4) * 2 + lax.rem(place[1] + dx, 2)
        out[pl.ds(pl.multiple_of(owner * count, count), count), :] = value[r * count : (r + 1) * count, :]


def weights_kernel(dist, scale, spots, out):
    scores = -dist[...] / scale[:, :1]
    top = jnp.max(scores, axis=1, keepdims=True)
    top_hi, top_lo = halves(top)
    weights = jnp.exp(scores - (top_hi + top_lo)).astype(BF16)
    tot_hi, tot_lo = halves(jnp.sum(weights.astype(F32), axis=1, keepdims=True))
    wide = spots.shape[1]
    out[:, :wide] = jnp.dot(weights, spots[...], preferred_element_type=F32).astype(BF16)
    out[:, wide:] = in_lanes((top_hi, top_lo, tot_hi, tot_lo)).astype(BF16)


def halves(value):
    first = value.astype(BF16).astype(F32)
    return first, (value - first).astype(BF16).astype(F32)


def in_lanes(columns):
    lane = lax.broadcasted_iota(jnp.int32, (columns[0].shape[0], 128), 1)
    value = columns[-1]
    for i in range(len(columns) - 2, -1, -1):
        value = jnp.where(lane == i, columns[i], value)
    return value


def compose_kernel(leads, place, own, up, down, perm, block, block_up, block_down, out):
    rows, quarter = block_up.shape
    targets, wide = own.shape[0], own.shape[1] - 128
    count = leads.shape[0]
    odd = lax.rem(place[0], 2)
    mixed, facts = [], []
    for w in (own, up, down):
        weights = w[:, :wide].astype(F32)
        stack = jnp.concatenate([pltpu.roll(weights, leads[k], 1) for k in range(count)], axis=0).astype(BF16)
        mixed.append(jnp.dot(perm[...], stack, preferred_element_type=F32).astype(BF16)[:, :rows])
        fact = jnp.concatenate([w[:, wide:]] * count, axis=0)
        facts.append(jnp.dot(perm[...], fact, preferred_element_type=F32))
    tops = [f[:, 0:1] + f[:, 1:2] for f in facts]
    totals = [f[:, 2:3] + f[:, 3:4] for f in facts]
    step = 512
    columns = []
    for side, (other, start) in enumerate(((block_up, 2 * odd), (block_down, 3 - 2 * odd))):
        i = side + 1
        larger = tops[0] >= tops[i]
        top = jnp.where(larger, tops[0], tops[i])
        first, second = jnp.exp(tops[0] - top), jnp.exp(tops[i] - top)
        columns += [jnp.where(larger, facts[0][:, j : j + 1], facts[i][:, j : j + 1]) for j in range(2)]
        columns += halves(first * totals[0] + second * totals[i])
        for c in range(0, quarter, step):
            mine = block[:, pl.ds(pl.multiple_of(start * quarter + c, step), step)]
            value = first * jnp.dot(mixed[0], mine, preferred_element_type=F32)
            value = value + second * jnp.dot(mixed[i], other[:, c : c + step], preferred_element_type=F32)
            out[:, side * quarter + c : side * quarter + c + step] = value.astype(BF16)
    out[:, 2 * quarter :] = in_lanes(columns).astype(BF16)


def combine_kernel(parts, out):
    n, rows, wide = parts.shape
    count, lead_n, width = out.shape
    quarter = width // 4
    facts = [parts[b, :, wide - 128 :].astype(F32) for b in range(n)]
    step = 512
    for q in range(4):
        odd, side = ((0, 0), (1, 1), (1, 0), (0, 1))[q]
        sources = [b for b in range(n) if (b // 2) % 2 == odd]
        at = 4 * side
        tops = [facts[b][:, at : at + 1] + facts[b][:, at + 1 : at + 2] for b in sources]
        top = functools.reduce(jnp.maximum, tops)
        factors = [jnp.exp(t - top) for t in tops]
        total = sum(f * (facts[b][:, at + 2 : at + 3] + facts[b][:, at + 3 : at + 4]) for f, b in zip(factors, sources))
        factors = [f / total for f in factors]
        for c in range(0, quarter, step):
            from_c = side * quarter + c
            summed = sum(f * parts[b, :, from_c : from_c + step].astype(F32) for f, b in zip(factors, sources))
            summed = summed.reshape(count, lead_n, step).astype(BF16)
            out[:, :, q * quarter + c : q * quarter + c + step] = summed


def total_over_space(value):
    value = value + lax.ppermute(value, "co", flip(2, 1))
    value = value + lax.ppermute(value, "xl", flip(2, 1))
    down = lax.ppermute(value, "z", turn(8, 1))
    up = lax.ppermute(value, "z", turn(8, -1))
    three, two = value + down + up, value + up
    high = lax.ppermute(three, "z", turn(8, -3))
    low = lax.ppermute(two, "z", turn(8, 3))
    return three + high + low


def per_device(targets, library, anchors, leads, spread):
    lags, count, width = targets.shape
    rows = library.shape[0]
    lead_n = leads.shape[0]
    n_lib = lax.axis_size(LIB)
    n_target = count * n_lib
    wide = -(-rows // 128) * 128
    scale = math.sqrt(lags * width * lax.axis_size(SPACE))
    quarter = width // 4

    near, away = gather_targets(targets.reshape(lags * count, width))

    y, xh = lax.axis_index(Y), lax.axis_index("xh")
    place = jnp.stack([y, xh]).astype(jnp.int32)
    norm = jnp.sum(jnp.square(library.astype(F32)), axis=1)
    norm = jnp.pad(norm, (0, wide - rows))
    lnorm = functools.reduce(jnp.add, [jnp.roll(norm, lag) for lag in range(lags)])
    lnorm = jnp.broadcast_to(lnorm[None, :], (8, wide))
    spots = lax.broadcasted_iota(jnp.int32, (anchors.shape[0], wide), 1)
    spots = (spots == anchors[:, None]).astype(BF16)
    picks = lax.broadcasted_iota(jnp.int32, (wide, anchors.shape[0]), 0)
    picks = (picks == anchors[None, :]).astype(BF16)
    scales = jnp.broadcast_to((spread * scale)[:, None], (n_target, 128))
    row = lax.broadcasted_iota(jnp.int32, (lead_n * n_target, lead_n * n_target), 0)
    col = lax.broadcasted_iota(jnp.int32, (lead_n * n_target, lead_n * n_target), 1)
    perm = ((row % lead_n) * n_target + row // lead_n == col).astype(BF16)

    flops = lags * n_target * wide * width
    near_dist = pl.pallas_call(
        functools.partial(near_kernel, lags),
        out_shape=jax.ShapeDtypeStruct((n_target // 2, wide), F32),
        in_specs=[VM] * 6,
        out_specs=VM,
        scratch_shapes=[pltpu.VMEM((lags * n_target // 2, wide), F32)],
        compiler_params=PARAMS,
        cost_estimate=pl.CostEstimate(flops=flops, bytes_accessed=5 << 20, transcendentals=0),
        name="near",
    )(*near, library, lnorm)
    partial_dist = pl.pallas_call(
        functools.partial(away_kernel, lags),
        out_shape=jax.ShapeDtypeStruct((n_target, anchors.shape[0]), F32),
        in_specs=[SM] + [VM] * 10,
        out_specs=VM,
        scratch_shapes=[pltpu.VMEM((lags * n_target // 2, wide), F32)],
        compiler_params=PARAMS,
        cost_estimate=pl.CostEstimate(flops=flops, bytes_accessed=5 << 20, transcendentals=0),
        name="away",
    )(place, *away, library, lnorm, near_dist, picks)

    odd = lax.rem(y, 2)
    for_up = lax.dynamic_slice_in_dim(library, (1 + 2 * odd) * quarter, quarter, axis=1)
    for_down = lax.dynamic_slice_in_dim(library, (2 - 2 * odd) * quarter, quarter, axis=1)
    for_up, for_down, partial_dist = lax.optimization_barrier((for_up, for_down, partial_dist))
    block_down = lax.ppermute(for_up, Y, turn(4, 1))
    block_up = lax.ppermute(for_down, Y, turn(4, -1))

    dist = total_over_space(partial_dist)
    own = pl.pallas_call(
        weights_kernel,
        out_shape=jax.ShapeDtypeStruct((n_target, wide + 128), BF16),
        in_specs=[VM] * 3,
        out_specs=VM,
        compiler_params=PARAMS,
        cost_estimate=pl.CostEstimate(flops=2 * n_target * wide * 256, bytes_accessed=1 << 20, transcendentals=n_target * 256),
        name="weights",
    )(dist, scales, spots)
    down = lax.ppermute(own, Y, turn(4, 1))
    up = lax.ppermute(own, Y, turn(4, -1))

    parts = pl.pallas_call(
        compose_kernel,
        out_shape=jax.ShapeDtypeStruct((lead_n * n_target, 2 * quarter + 128), BF16),
        in_specs=[SM] * 2 + [VM] * 7,
        out_specs=VM,
        compiler_params=PARAMS,
        cost_estimate=pl.CostEstimate(flops=2 * lead_n * n_target * rows * width, bytes_accessed=5 << 20, transcendentals=n_target * wide),
        name="compose",
    )(leads, place, own, up, down, perm, library, block_up, block_down)

    parts = parts.reshape(n_lib, lead_n * count, 2 * quarter + 128)
    parts = lax.all_to_all(parts, LIB, 0, 0, tiled=True)

    return pl.pallas_call(
        combine_kernel,
        out_shape=jax.ShapeDtypeStruct((count, lead_n, width), BF16),
        in_specs=[VM],
        out_specs=VM,
        compiler_params=PARAMS,
        cost_estimate=pl.CostEstimate(flops=2 * n_target * lead_n * width, bytes_accessed=3 << 20, transcendentals=0),
        name="combine",
    )(parts)


def solution(mesh):
    fine = Mesh(mesh.devices.reshape(8, 2, 2, 2, 2, 2), SPACE + LIB)
    placed = (P(None, LIB, SPACE), P(LIB, SPACE), P(LIB), P(), P())
    return jax.shard_map(per_device, mesh=fine, in_specs=placed, out_specs=P(LIB, None, SPACE), check_vma=False)
```

```python
import functools
import math

import jax
import jax.numpy as jnp
from jax import lax
from jax.experimental import pallas as pl
from jax.experimental.pallas import tpu as pltpu
from jax.sharding import Mesh, PartitionSpec as P

F32 = jnp.float32
BF16 = jnp.bfloat16
Y = ("yh", "yl")
LIB = ("yh", "yl", "xh")
SPACE = ("z", "xl", "co")
VM = pl.BlockSpec(memory_space=pltpu.VMEM)
SM = pl.BlockSpec(memory_space=pltpu.SMEM)
PARAMS = pltpu.CompilerParams(vmem_limit_bytes=16 * 1024 * 1024)
NEAR = ((0, 0), (0, 1), (3, 0), (1, 0))
AWAY = ((3, 1), (1, 1), (2, 0), (2, 1))


def flip(n, bit):
    return [(i, i ^ bit) for i in range(n)]


def turn(n, by):
    return [(i, (i + by) % n) for i in range(n)]


def gather_targets(targets):
    lags, count, width = targets.shape
    own = targets.reshape(lags * count, width)
    half = lags * count // 2
    early, late = own[:half], own[half:]
    across = lax.ppermute(own, "xh", flip(2, 1))
    below_a = lax.ppermute(early, Y, turn(4, 1))
    above_b = lax.ppermute(late, Y, turn(4, -1))
    below_b = lax.ppermute(late, Y, turn(4, 1))
    above_a = lax.ppermute(early, Y, turn(4, -1))
    far_a = lax.ppermute(below_a, Y, turn(4, 1))
    far_b = lax.ppermute(above_b, Y, turn(4, -1))
    across, below_b, above_a = lax.optimization_barrier((across, below_b, above_a))
    below_x = lax.ppermute(across, Y, turn(4, 1))
    above_x = lax.ppermute(across, Y, turn(4, -1))
    far_xa = lax.ppermute(far_a, "xh", flip(2, 1))
    far_xb = lax.ppermute(far_b, "xh", flip(2, 1))
    return (own, across, below_a, below_b, above_a, above_b), (below_x, above_x, far_a, far_b, far_xa, far_xb)


def place_on_y():
    return lax.axis_index("yh") * 2 + lax.axis_index("yl")


def prepare_kernel(lags, factor, library, anchors, spread, lnorm, picks, scale, for_up, for_down):
    rows, width = library.shape
    wide = picks.shape[0]
    squares = jnp.zeros((rows, 128), F32)
    for c in range(0, width, 128):
        part = library[:, c : c + 128].astype(F32)
        squares = squares + part * part
    squares = jnp.concatenate([squares, jnp.zeros((wide - rows, 128), F32)], axis=0)
    norm = jnp.sum(squares.T, axis=0, keepdims=True)
    norm = jnp.broadcast_to(norm, lnorm.shape)
    total = norm
    for lag in range(1, lags):
        total = total + pltpu.roll(norm, lag, 1)
    lnorm[...] = total
    spots = lax.broadcasted_iota(jnp.int32, picks.shape, 0)
    picks[...] = jnp.where(spots == anchors[...], 1.0, 0.0).astype(BF16)
    count = scale.shape[0]
    wider = jnp.concatenate([spread[...] * factor, jnp.ones((1, 128 - count), F32)], axis=1)
    scale[...] = jnp.broadcast_to(wider, (128, 128)).T[:count, :]
    quarter = for_up.shape[1]
    odd = lax.axis_index("yl")
    for_up[...] = library[:, pl.ds(pl.multiple_of((1 + 2 * odd) * quarter, quarter), quarter)]
    for_down[...] = library[:, pl.ds(pl.multiple_of((2 - 2 * odd) * quarter, quarter), quarter)]


def cross_rows(lags, pieces, block, lnorm, acc):
    rows, width = block.shape
    acc[...] = jnp.zeros_like(acc)
    lhs = jnp.concatenate([p[...] for p in pieces], axis=0)
    acc[:, :rows] = lax.dot_general(lhs, block[...], (((1,), (1,)), ((), ())), preferred_element_type=F32)
    norms = jnp.zeros((acc.shape[0], 128), F32)
    for c in range(0, width, 128):
        part = lhs[:, c : c + 128].astype(F32)
        norms = norms + part * part
    norms = jnp.sum(norms, axis=1, keepdims=True)
    count = acc.shape[0] // 4 // lags
    values = []
    for r in range(4):
        cross = jnp.zeros((count, acc.shape[1]), F32)
        tnorm = jnp.zeros((count, 1), F32)
        for lag in range(lags):
            at = (r * lags + lag) * count
            here = acc[at : at + count, :]
            cross = cross + (pltpu.roll(here, lag, 1) if lag else here)
            tnorm = tnorm + norms[at : at + count]
        values.append(tnorm + lnorm[:1, :] - 2.0 * cross)
    return values


def at_anchors(value, picks):
    first = value.astype(BF16)
    rest = value - first.astype(F32)
    second = rest.astype(BF16)
    third = (rest - second.astype(F32)).astype(BF16)
    parts = jnp.concatenate([first, second, third], axis=0)
    parts = jnp.dot(parts, picks[...], preferred_element_type=F32)
    n = value.shape[0]
    return parts[:n] + parts[n : 2 * n] + parts[2 * n :]


def near_kernel(lags, *refs):
    pieces, (block, lnorm, picks, out, acc) = refs[:6], refs[6:]
    values = cross_rows(lags, pieces, block, lnorm, acc)
    out[...] = at_anchors(jnp.concatenate(values, axis=0), picks)


def away_kernel(lags, *refs):
    pieces, (block, lnorm, picks, near, out, acc) = refs[:6], refs[6:]
    values = cross_rows(lags, pieces, block, lnorm, acc)
    count = values[0].shape[0]
    value = at_anchors(jnp.concatenate(values, axis=0), picks)
    y, xh = place_on_y(), lax.axis_index("xh")
    for r, (dy, dx) in enumerate(NEAR + AWAY):
        owner = lax.rem(y + dy, 4) * 2 + lax.rem(xh + dx, 2)
        source, at = (near, r) if r < 4 else (value, r - 4)
        out[pl.ds(pl.multiple_of(owner * count, count), count), :] = source[at * count : (at + 1) * count, :]


def weights_kernel(dist, scale, picks, out):
    scores = -dist[...] / scale[:, :1]
    top = jnp.max(scores, axis=1, keepdims=True)
    top_hi, top_lo = halves(top)
    weights = jnp.exp(scores - (top_hi + top_lo)).astype(BF16)
    tot_hi, tot_lo = halves(jnp.sum(weights.astype(F32), axis=1, keepdims=True))
    wide = picks.shape[0]
    spread_out = lax.dot_general(weights, picks[...], (((1,), (1,)), ((), ())), preferred_element_type=F32)
    out[:, :wide] = spread_out.astype(BF16)
    out[:, wide:] = in_lanes((top_hi, top_lo, tot_hi, tot_lo)).astype(BF16)


def halves(value):
    first = value.astype(BF16).astype(F32)
    return first, (value - first).astype(BF16).astype(F32)


def in_lanes(columns):
    lane = lax.broadcasted_iota(jnp.int32, (columns[0].shape[0], 128), 1)
    value = columns[-1]
    for i in range(len(columns) - 2, -1, -1):
        value = jnp.where(lane == i, columns[i], value)
    return value


def compose_kernel(leads, own, up, down, block, block_up, block_down, out):
    rows, quarter = block_up.shape
    targets, wide = own.shape[0], own.shape[1] - 128
    count = leads.shape[0]
    odd = lax.axis_index("yl")
    shape = (count * targets, count * targets)
    row, col = lax.broadcasted_iota(jnp.int32, shape, 0), lax.broadcasted_iota(jnp.int32, shape, 1)
    perm = jnp.where(lax.rem(row, count) * targets + lax.div(row, count) == col, 1.0, 0.0).astype(BF16)
    mixed, facts = [], []
    for w in (own, up, down):
        weights = w[:, :wide].astype(F32)
        stack = jnp.concatenate([pltpu.roll(weights, leads[k], 1) for k in range(count)], axis=0).astype(BF16)
        mixed.append(jnp.dot(perm, stack, preferred_element_type=F32).astype(BF16)[:, :rows])
        fact = jnp.concatenate([w[:, wide:]] * count, axis=0)
        facts.append(jnp.dot(perm, fact, preferred_element_type=F32))
    tops = [f[:, 0:1] + f[:, 1:2] for f in facts]
    totals = [f[:, 2:3] + f[:, 3:4] for f in facts]
    step = 512
    columns = []
    for side, (other, start) in enumerate(((block_up, 2 * odd), (block_down, 3 - 2 * odd))):
        i = side + 1
        larger = tops[0] >= tops[i]
        top = jnp.where(larger, tops[0], tops[i])
        first, second = jnp.exp(tops[0] - top), jnp.exp(tops[i] - top)
        columns += [jnp.where(larger, facts[0][:, j : j + 1], facts[i][:, j : j + 1]) for j in range(2)]
        columns += halves(first * totals[0] + second * totals[i])
        for c in range(0, quarter, step):
            mine = block[:, pl.ds(pl.multiple_of(start * quarter + c, step), step)]
            value = first * jnp.dot(mixed[0], mine, preferred_element_type=F32)
            value = value + second * jnp.dot(mixed[i], other[:, c : c + step], preferred_element_type=F32)
            out[:, side * quarter + c : side * quarter + c + step] = value.astype(BF16)
    out[:, 2 * quarter :] = in_lanes(columns).astype(BF16)


def combine_kernel(parts, out):
    n, rows, wide = parts.shape
    count, lead_n, width = out.shape
    quarter = width // 4
    facts = [parts[b, :, wide - 128 :].astype(F32) for b in range(n)]
    step = 512
    for q in range(4):
        odd, side = ((0, 0), (1, 1), (1, 0), (0, 1))[q]
        sources = [b for b in range(n) if (b // 2) % 2 == odd]
        at = 4 * side
        tops = [facts[b][:, at : at + 1] + facts[b][:, at + 1 : at + 2] for b in sources]
        top = functools.reduce(jnp.maximum, tops)
        factors = [jnp.exp(t - top) for t in tops]
        total = sum(f * (facts[b][:, at + 2 : at + 3] + facts[b][:, at + 3 : at + 4]) for f, b in zip(factors, sources))
        factors = [f / total for f in factors]
        for c in range(0, quarter, step):
            from_c = side * quarter + c
            summed = sum(f * parts[b, :, from_c : from_c + step].astype(F32) for f, b in zip(factors, sources))
            summed = summed.reshape(count, lead_n, step).astype(BF16)
            out[:, :, q * quarter + c : q * quarter + c + step] = summed


def total_over_space(value):
    value = value + lax.ppermute(value, "co", flip(2, 1))
    value = value + lax.ppermute(value, "xl", flip(2, 1))
    down = lax.ppermute(value, "z", turn(8, 1))
    up = lax.ppermute(value, "z", turn(8, -1))
    three, two = value + down + up, value + up
    high = lax.ppermute(three, "z", turn(8, -3))
    low = lax.ppermute(two, "z", turn(8, 3))
    return three + high + low


def per_device(targets, library, anchors, leads, spread):
    lags, count, width = targets.shape
    rows = library.shape[0]
    lead_n = leads.shape[0]
    n_lib = lax.axis_size(LIB)
    n_target = count * n_lib
    wide = -(-rows // 128) * 128
    scale = math.sqrt(lags * width * lax.axis_size(SPACE))
    quarter = width // 4

    near, away = gather_targets(targets)

    n_anchor = anchors.shape[0]
    lnorm, picks, scales, for_up, for_down = pl.pallas_call(
        functools.partial(prepare_kernel, lags, scale),
        out_shape=(
            jax.ShapeDtypeStruct((8, wide), F32),
            jax.ShapeDtypeStruct((wide, n_anchor), BF16),
            jax.ShapeDtypeStruct((n_target, 128), F32),
            jax.ShapeDtypeStruct((rows, quarter), BF16),
            jax.ShapeDtypeStruct((rows, quarter), BF16),
        ),
        in_specs=[VM] * 3,
        out_specs=(VM,) * 5,
        compiler_params=PARAMS,
        cost_estimate=pl.CostEstimate(flops=2 * rows * width, bytes_accessed=4 << 20, transcendentals=0),
        name="prepare",
    )(library, anchors.reshape(1, n_anchor), spread.reshape(1, n_target))

    flops = lags * n_target * wide * width
    near_dist = pl.pallas_call(
        functools.partial(near_kernel, lags),
        out_shape=jax.ShapeDtypeStruct((n_target // 2, n_anchor), F32),
        in_specs=[VM] * 9,
        out_specs=VM,
        scratch_shapes=[pltpu.VMEM((lags * n_target // 2, wide), F32)],
        compiler_params=PARAMS,
        cost_estimate=pl.CostEstimate(flops=flops, bytes_accessed=5 << 20, transcendentals=0),
        name="near",
    )(*near, library, lnorm, picks)

    for_up, for_down, near_dist = lax.optimization_barrier((for_up, for_down, near_dist))
    block_down = lax.ppermute(for_up, Y, turn(4, 1))
    block_up = lax.ppermute(for_down, Y, turn(4, -1))

    partial_dist = pl.pallas_call(
        functools.partial(away_kernel, lags),
        out_shape=jax.ShapeDtypeStruct((n_target, n_anchor), F32),
        in_specs=[VM] * 10,
        out_specs=VM,
        scratch_shapes=[pltpu.VMEM((lags * n_target // 2, wide), F32)],
        compiler_params=PARAMS,
        cost_estimate=pl.CostEstimate(flops=flops, bytes_accessed=5 << 20, transcendentals=0),
        name="away",
    )(*away, library, lnorm, picks, near_dist)

    dist = total_over_space(partial_dist)
    own = pl.pallas_call(
        weights_kernel,
        out_shape=jax.ShapeDtypeStruct((n_target, wide + 128), BF16),
        in_specs=[VM] * 3,
        out_specs=VM,
        compiler_params=PARAMS,
        cost_estimate=pl.CostEstimate(flops=2 * n_target * wide * 256, bytes_accessed=1 << 20, transcendentals=n_target * 256),
        name="weights",
    )(dist, scales, picks)
    down = lax.ppermute(own, Y, turn(4, 1))
    up = lax.ppermute(own, Y, turn(4, -1))

    parts = pl.pallas_call(
        compose_kernel,
        out_shape=jax.ShapeDtypeStruct((lead_n * n_target, 2 * quarter + 128), BF16),
        in_specs=[SM] + [VM] * 6,
        out_specs=VM,
        compiler_params=PARAMS,
        cost_estimate=pl.CostEstimate(flops=2 * lead_n * n_target * rows * width, bytes_accessed=5 << 20, transcendentals=n_target * wide),
        name="compose",
    )(leads, own, up, down, library, block_up, block_down)

    parts = parts.reshape(n_lib, lead_n * count, 2 * quarter + 128)
    parts = lax.all_to_all(parts, LIB, 0, 0, tiled=True)

    return pl.pallas_call(
        combine_kernel,
        out_shape=jax.ShapeDtypeStruct((count, lead_n, width), BF16),
        in_specs=[VM],
        out_specs=VM,
        compiler_params=PARAMS,
        cost_estimate=pl.CostEstimate(flops=2 * n_target * lead_n * width, bytes_accessed=3 << 20, transcendentals=0),
        name="combine",
    )(parts)


def solution(mesh):
    fine = Mesh(mesh.devices.reshape(8, 2, 2, 2, 2, 2), SPACE + LIB)
    placed = (P(None, LIB, SPACE), P(LIB, SPACE), P(LIB), P(), P())
    return jax.shard_map(per_device, mesh=fine, in_specs=placed, out_specs=P(LIB, None, SPACE), check_vma=False)
```

```python
import functools
import math

import jax
import jax.numpy as jnp
from jax import lax
from jax.experimental import pallas as pl
from jax.experimental.pallas import tpu as pltpu
from jax.sharding import Mesh, PartitionSpec as P

F32 = jnp.float32
BF16 = jnp.bfloat16
Y = ("yh", "yl")
LIB = ("yh", "yl", "xh")
SPACE = ("z", "xl", "co")
VM = pl.BlockSpec(memory_space=pltpu.VMEM)
SM = pl.BlockSpec(memory_space=pltpu.SMEM)
PARAMS = pltpu.CompilerParams(vmem_limit_bytes=16 * 1024 * 1024)
NEAR = ((0, 0), (0, 1), (3, 0), (1, 0))
AWAY = ((3, 1), (1, 1), (2, 0), (2, 1))


def flip(n, bit):
    return [(i, i ^ bit) for i in range(n)]


def turn(n, by):
    return [(i, (i + by) % n) for i in range(n)]


def gather_targets(targets, ready):
    lags, count, width = targets.shape
    own = targets.reshape(lags * count, width)
    half = lags * count // 2
    early, late = own[:half], own[half:]
    across = lax.ppermute(own, "xh", flip(2, 1))
    below_a = lax.ppermute(early, Y, turn(4, 1))
    above_b = lax.ppermute(late, Y, turn(4, -1))
    below_b = lax.ppermute(late, Y, turn(4, 1))
    above_a = lax.ppermute(early, Y, turn(4, -1))
    below_a, above_b, ready = lax.optimization_barrier((below_a, above_b, ready))
    far_a = lax.ppermute(below_a, Y, turn(4, 1))
    far_b = lax.ppermute(above_b, Y, turn(4, -1))
    across, below_b, above_a = lax.optimization_barrier((across, below_b, above_a))
    below_x = lax.ppermute(across, Y, turn(4, 1))
    above_x = lax.ppermute(across, Y, turn(4, -1))
    far_xa = lax.ppermute(far_a, "xh", flip(2, 1))
    far_xb = lax.ppermute(far_b, "xh", flip(2, 1))
    return (own, across, below_a, below_b, above_a, above_b), (below_x, above_x, far_a, far_b, far_xa, far_xb), ready


def place_on_y():
    return lax.axis_index("yh") * 2 + lax.axis_index("yl")


def prepare_kernel(lags, factor, library, anchors, spread, lnorm, picks, scale, for_up, for_down):
    rows, width = library.shape
    wide = picks.shape[0]
    squares = jnp.zeros((rows, 128), F32)
    for c in range(0, width, 128):
        part = library[:, c : c + 128].astype(F32)
        squares = squares + part * part
    squares = jnp.concatenate([squares, jnp.zeros((wide - rows, 128), F32)], axis=0)
    norm = jnp.sum(squares.T, axis=0, keepdims=True)
    norm = jnp.broadcast_to(norm, lnorm.shape)
    total = norm
    for lag in range(1, lags):
        total = total + pltpu.roll(norm, lag, 1)
    lnorm[...] = total
    spots = lax.broadcasted_iota(jnp.int32, picks.shape, 0)
    picks[...] = jnp.where(spots == anchors[...], 1.0, 0.0).astype(BF16)
    count = scale.shape[0]
    wider = jnp.concatenate([spread[...] * factor, jnp.ones((1, 128 - count), F32)], axis=1)
    scale[...] = jnp.broadcast_to(wider, (128, 128)).T[:count, :]
    quarter = for_up.shape[1]
    odd = lax.axis_index("yl")
    for_up[...] = library[:, pl.ds(pl.multiple_of((1 + 2 * odd) * quarter, quarter), quarter)]
    for_down[...] = library[:, pl.ds(pl.multiple_of((2 - 2 * odd) * quarter, quarter), quarter)]


def cross_rows(lags, pieces, block, lnorm, acc):
    rows, width = block.shape
    acc[...] = jnp.zeros_like(acc)
    lhs = jnp.concatenate([p[...] for p in pieces], axis=0)
    acc[:, :rows] = lax.dot_general(lhs, block[...], (((1,), (1,)), ((), ())), preferred_element_type=F32)
    norms = jnp.zeros((acc.shape[0], 128), F32)
    for c in range(0, width, 128):
        part = lhs[:, c : c + 128].astype(F32)
        norms = norms + part * part
    norms = jnp.sum(norms, axis=1, keepdims=True)
    count = acc.shape[0] // 4 // lags
    values = []
    for r in range(4):
        cross = jnp.zeros((count, acc.shape[1]), F32)
        tnorm = jnp.zeros((count, 1), F32)
        for lag in range(lags):
            at = (r * lags + lag) * count
            here = acc[at : at + count, :]
            cross = cross + (pltpu.roll(here, lag, 1) if lag else here)
            tnorm = tnorm + norms[at : at + count]
        values.append(tnorm + lnorm[:1, :] - 2.0 * cross)
    return values


def at_anchors(value, picks):
    first = value.astype(BF16)
    rest = value - first.astype(F32)
    second = rest.astype(BF16)
    third = (rest - second.astype(F32)).astype(BF16)
    parts = jnp.concatenate([first, second, third], axis=0)
    parts = jnp.dot(parts, picks[...], preferred_element_type=F32)
    n = value.shape[0]
    return parts[:n] + parts[n : 2 * n] + parts[2 * n :]


def near_kernel(lags, *refs):
    pieces, (block, lnorm, picks, out, acc) = refs[:6], refs[6:]
    values = cross_rows(lags, pieces, block, lnorm, acc)
    out[...] = at_anchors(jnp.concatenate(values, axis=0), picks)


def away_kernel(lags, *refs):
    pieces, (block, lnorm, picks, near, out, acc) = refs[:6], refs[6:]
    values = cross_rows(lags, pieces, block, lnorm, acc)
    count = values[0].shape[0]
    value = at_anchors(jnp.concatenate(values, axis=0), picks)
    y, xh = place_on_y(), lax.axis_index("xh")
    for r, (dy, dx) in enumerate(NEAR + AWAY):
        owner = lax.rem(y + dy, 4) * 2 + lax.rem(xh + dx, 2)
        source, at = (near, r) if r < 4 else (value, r - 4)
        out[pl.ds(pl.multiple_of(owner * count, count), count), :] = source[at * count : (at + 1) * count, :]


def weights_kernel(dist, scale, picks, out):
    scores = -dist[...] / scale[:, :1]
    top = jnp.max(scores, axis=1, keepdims=True)
    top_hi, top_lo = halves(top)
    weights = jnp.exp(scores - (top_hi + top_lo)).astype(BF16)
    tot_hi, tot_lo = halves(jnp.sum(weights.astype(F32), axis=1, keepdims=True))
    wide = picks.shape[0]
    spread_out = lax.dot_general(weights, picks[...], (((1,), (1,)), ((), ())), preferred_element_type=F32)
    out[:, :wide] = spread_out.astype(BF16)
    out[:, wide:] = in_lanes((top_hi, top_lo, tot_hi, tot_lo)).astype(BF16)


def halves(value):
    first = value.astype(BF16).astype(F32)
    return first, (value - first).astype(BF16).astype(F32)


def in_lanes(columns):
    lane = lax.broadcasted_iota(jnp.int32, (columns[0].shape[0], 128), 1)
    value = columns[-1]
    for i in range(len(columns) - 2, -1, -1):
        value = jnp.where(lane == i, columns[i], value)
    return value


def compose_kernel(leads, own, up, down, block, block_up, block_down, out):
    rows, quarter = block_up.shape
    targets, wide = own.shape[0], own.shape[1] - 128
    count = leads.shape[0]
    odd = lax.axis_index("yl")
    shape = (count * targets, count * targets)
    row, col = lax.broadcasted_iota(jnp.int32, shape, 0), lax.broadcasted_iota(jnp.int32, shape, 1)
    perm = jnp.where(lax.rem(row, count) * targets + lax.div(row, count) == col, 1.0, 0.0).astype(BF16)
    mixed, facts = [], []
    for w in (own, up, down):
        weights = w[:, :wide].astype(F32)
        stack = jnp.concatenate([pltpu.roll(weights, leads[k], 1) for k in range(count)], axis=0).astype(BF16)
        mixed.append(jnp.dot(perm, stack, preferred_element_type=F32).astype(BF16)[:, :rows])
        fact = jnp.concatenate([w[:, wide:]] * count, axis=0)
        facts.append(jnp.dot(perm, fact, preferred_element_type=F32))
    tops = [f[:, 0:1] + f[:, 1:2] for f in facts]
    totals = [f[:, 2:3] + f[:, 3:4] for f in facts]
    step = 512
    columns = []
    for side, (other, start) in enumerate(((block_up, 2 * odd), (block_down, 3 - 2 * odd))):
        i = side + 1
        larger = tops[0] >= tops[i]
        top = jnp.where(larger, tops[0], tops[i])
        first, second = jnp.exp(tops[0] - top), jnp.exp(tops[i] - top)
        columns += [jnp.where(larger, facts[0][:, j : j + 1], facts[i][:, j : j + 1]) for j in range(2)]
        columns += halves(first * totals[0] + second * totals[i])
        for c in range(0, quarter, step):
            mine = block[:, pl.ds(pl.multiple_of(start * quarter + c, step), step)]
            value = first * jnp.dot(mixed[0], mine, preferred_element_type=F32)
            value = value + second * jnp.dot(mixed[i], other[:, c : c + step], preferred_element_type=F32)
            out[:, side * quarter + c : side * quarter + c + step] = value.astype(BF16)
    out[:, 2 * quarter :] = in_lanes(columns).astype(BF16)


def combine_kernel(parts, out):
    n, rows, wide = parts.shape
    count, lead_n, width = out.shape
    quarter = width // 4
    facts = [parts[b, :, wide - 128 :].astype(F32) for b in range(n)]
    step = 512
    for q in range(4):
        odd, side = ((0, 0), (1, 1), (1, 0), (0, 1))[q]
        sources = [b for b in range(n) if (b // 2) % 2 == odd]
        at = 4 * side
        tops = [facts[b][:, at : at + 1] + facts[b][:, at + 1 : at + 2] for b in sources]
        top = functools.reduce(jnp.maximum, tops)
        factors = [jnp.exp(t - top) for t in tops]
        total = sum(f * (facts[b][:, at + 2 : at + 3] + facts[b][:, at + 3 : at + 4]) for f, b in zip(factors, sources))
        factors = [f / total for f in factors]
        for c in range(0, quarter, step):
            from_c = side * quarter + c
            summed = sum(f * parts[b, :, from_c : from_c + step].astype(F32) for f, b in zip(factors, sources))
            summed = summed.reshape(count, lead_n, step).astype(BF16)
            out[:, :, q * quarter + c : q * quarter + c + step] = summed


def total_over_space(value, arriving):
    value = value + lax.ppermute(value, "co", flip(2, 1))
    value = value + lax.ppermute(value, "xl", flip(2, 1))
    down = lax.ppermute(value, "z", turn(8, 1))
    up = lax.ppermute(value, "z", turn(8, -1))
    three, two = value + down + up, value + up
    three, two, arriving = lax.optimization_barrier((three, two, arriving))
    high = lax.ppermute(three, "z", turn(8, -3))
    low = lax.ppermute(two, "z", turn(8, 3))
    return three + high + low, arriving


def per_device(targets, library, anchors, leads, spread):
    lags, count, width = targets.shape
    rows = library.shape[0]
    lead_n = leads.shape[0]
    n_lib = lax.axis_size(LIB)
    n_target = count * n_lib
    wide = -(-rows // 128) * 128
    scale = math.sqrt(lags * width * lax.axis_size(SPACE))
    quarter = width // 4

    n_anchor = anchors.shape[0]
    ready = pl.pallas_call(
        functools.partial(prepare_kernel, lags, scale),
        out_shape=(
            jax.ShapeDtypeStruct((8, wide), F32),
            jax.ShapeDtypeStruct((wide, n_anchor), BF16),
            jax.ShapeDtypeStruct((n_target, 128), F32),
            jax.ShapeDtypeStruct((rows, quarter), BF16),
            jax.ShapeDtypeStruct((rows, quarter), BF16),
        ),
        in_specs=[VM] * 3,
        out_specs=(VM,) * 5,
        compiler_params=PARAMS,
        cost_estimate=pl.CostEstimate(flops=2 * rows * width, bytes_accessed=4 << 20, transcendentals=0),
        name="prepare",
    )(library, anchors.reshape(1, n_anchor), spread.reshape(1, n_target))
    near, away, ready = gather_targets(targets, ready)
    lnorm, picks, scales, for_up, for_down = ready

    flops = lags * n_target * wide * width
    near_dist = pl.pallas_call(
        functools.partial(near_kernel, lags),
        out_shape=jax.ShapeDtypeStruct((n_target // 2, n_anchor), F32),
        in_specs=[VM] * 9,
        out_specs=VM,
        scratch_shapes=[pltpu.VMEM((lags * n_target // 2, wide), F32)],
        compiler_params=PARAMS,
        cost_estimate=pl.CostEstimate(flops=flops, bytes_accessed=5 << 20, transcendentals=0),
        name="near",
    )(*near, library, lnorm, picks)

    for_up, for_down, near_dist = lax.optimization_barrier((for_up, for_down, near_dist))
    block_down = lax.ppermute(for_up, Y, turn(4, 1))
    block_up = lax.ppermute(for_down, Y, turn(4, -1))

    partial_dist = pl.pallas_call(
        functools.partial(away_kernel, lags),
        out_shape=jax.ShapeDtypeStruct((n_target, n_anchor), F32),
        in_specs=[VM] * 10,
        out_specs=VM,
        scratch_shapes=[pltpu.VMEM((lags * n_target // 2, wide), F32)],
        compiler_params=PARAMS,
        cost_estimate=pl.CostEstimate(flops=flops, bytes_accessed=5 << 20, transcendentals=0),
        name="away",
    )(*away, library, lnorm, picks, near_dist)

    dist, (block_up, block_down) = total_over_space(partial_dist, (block_up, block_down))
    own = pl.pallas_call(
        weights_kernel,
        out_shape=jax.ShapeDtypeStruct((n_target, wide + 128), BF16),
        in_specs=[VM] * 3,
        out_specs=VM,
        compiler_params=PARAMS,
        cost_estimate=pl.CostEstimate(flops=2 * n_target * wide * 256, bytes_accessed=1 << 20, transcendentals=n_target * 256),
        name="weights",
    )(dist, scales, picks)
    down = lax.ppermute(own, Y, turn(4, 1))
    up = lax.ppermute(own, Y, turn(4, -1))

    parts = pl.pallas_call(
        compose_kernel,
        out_shape=jax.ShapeDtypeStruct((lead_n * n_target, 2 * quarter + 128), BF16),
        in_specs=[SM] + [VM] * 6,
        out_specs=VM,
        compiler_params=PARAMS,
        cost_estimate=pl.CostEstimate(flops=2 * lead_n * n_target * rows * width, bytes_accessed=5 << 20, transcendentals=n_target * wide),
        name="compose",
    )(leads, own, up, down, library, block_up, block_down)

    parts = parts.reshape(n_lib, lead_n * count, 2 * quarter + 128)
    parts = lax.all_to_all(parts, LIB, 0, 0, tiled=True)

    return pl.pallas_call(
        combine_kernel,
        out_shape=jax.ShapeDtypeStruct((count, lead_n, width), BF16),
        in_specs=[VM],
        out_specs=VM,
        compiler_params=PARAMS,
        cost_estimate=pl.CostEstimate(flops=2 * n_target * lead_n * width, bytes_accessed=3 << 20, transcendentals=0),
        name="combine",
    )(parts)


def solution(mesh):
    fine = Mesh(mesh.devices.reshape(8, 2, 2, 2, 2, 2), SPACE + LIB)
    placed = (P(None, LIB, SPACE), P(LIB, SPACE), P(LIB), P(), P())
    return jax.shard_map(per_device, mesh=fine, in_specs=placed, out_specs=P(LIB, None, SPACE), check_vma=False)
```

```python
import functools
import math

import jax
import jax.numpy as jnp
from jax import lax
from jax.experimental import pallas as pl
from jax.experimental.pallas import tpu as pltpu
from jax.sharding import Mesh, PartitionSpec as P

F32 = jnp.float32
BF16 = jnp.bfloat16
Y = ("yh", "yl")
LIB = ("yh", "yl", "xh")
SPACE = ("z", "xl", "co")
VM = pl.BlockSpec(memory_space=pltpu.VMEM)
SM = pl.BlockSpec(memory_space=pltpu.SMEM)
PARAMS = pltpu.CompilerParams(vmem_limit_bytes=16 * 1024 * 1024)
NEAR = ((0, 0), (0, 1), (3, 0), (1, 0))
AWAY = ((3, 1), (1, 1), (2, 0), (2, 1))


def flip(n, bit):
    return [(i, i ^ bit) for i in range(n)]


def turn(n, by):
    return [(i, (i + by) % n) for i in range(n)]


def gather_targets(targets, ready):
    lags, count, width = targets.shape
    own = targets.reshape(lags * count, width)
    half = lags * count // 2
    early, late = own[:half], own[half:]
    across = lax.ppermute(own, "xh", flip(2, 1))
    below_a = lax.ppermute(early, Y, turn(4, 1))
    above_b = lax.ppermute(late, Y, turn(4, -1))
    below_b = lax.ppermute(late, Y, turn(4, 1))
    above_a = lax.ppermute(early, Y, turn(4, -1))
    below_a, above_b, ready = lax.optimization_barrier((below_a, above_b, ready))
    far_a = lax.ppermute(below_a, Y, turn(4, 1))
    far_b = lax.ppermute(above_b, Y, turn(4, -1))
    across, below_b, above_a = lax.optimization_barrier((across, below_b, above_a))
    below_x = lax.ppermute(across, Y, turn(4, 1))
    above_x = lax.ppermute(across, Y, turn(4, -1))
    far_xa = lax.ppermute(far_a, "xh", flip(2, 1))
    far_xb = lax.ppermute(far_b, "xh", flip(2, 1))
    return (own, across, below_a, below_b, above_a, above_b), (below_x, above_x, far_a, far_b, far_xa, far_xb), ready


def place_on_y():
    return lax.axis_index("yh") * 2 + lax.axis_index("yl")


def prepare_kernel(lags, factor, library, anchors, spread, lnorm, picks, scale, for_up, for_down):
    rows, width = library.shape
    wide = picks.shape[0]
    squares = jnp.zeros((rows, 128), F32)
    for c in range(0, width, 128):
        part = library[:, c : c + 128].astype(F32)
        squares = squares + part * part
    squares = jnp.concatenate([squares, jnp.zeros((wide - rows, 128), F32)], axis=0)
    norm = jnp.sum(squares.T, axis=0, keepdims=True)
    norm = jnp.broadcast_to(norm, lnorm.shape)
    total = norm
    for lag in range(1, lags):
        total = total + pltpu.roll(norm, lag, 1)
    lnorm[...] = total
    spots = lax.broadcasted_iota(jnp.int32, picks.shape, 0)
    picks[...] = jnp.where(spots == anchors[...], 1.0, 0.0).astype(BF16)
    count = scale.shape[0]
    wider = jnp.concatenate([spread[...] * factor, jnp.ones((1, 128 - count), F32)], axis=1)
    scale[...] = jnp.broadcast_to(wider, (128, 128)).T[:count, :]
    quarter = for_up.shape[1]
    odd = lax.axis_index("yl")
    for_up[...] = library[:, pl.ds(pl.multiple_of((1 + 2 * odd) * quarter, quarter), quarter)]
    for_down[...] = library[:, pl.ds(pl.multiple_of((2 - 2 * odd) * quarter, quarter), quarter)]


def cross_rows(lags, pieces, block, lnorm, acc):
    rows, width = block.shape
    acc[...] = jnp.zeros_like(acc)
    lhs = jnp.concatenate([p[...] for p in pieces], axis=0)
    acc[:, :rows] = lax.dot_general(lhs, block[...], (((1,), (1,)), ((), ())), preferred_element_type=F32)
    norms = jnp.zeros((acc.shape[0], 128), F32)
    for c in range(0, width, 128):
        part = lhs[:, c : c + 128].astype(F32)
        norms = norms + part * part
    norms = jnp.sum(norms, axis=1, keepdims=True)
    count = acc.shape[0] // 4 // lags
    values = []
    for r in range(4):
        cross = jnp.zeros((count, acc.shape[1]), F32)
        tnorm = jnp.zeros((count, 1), F32)
        for lag in range(lags):
            at = (r * lags + lag) * count
            here = acc[at : at + count, :]
            cross = cross + (pltpu.roll(here, lag, 1) if lag else here)
            tnorm = tnorm + norms[at : at + count]
        values.append(tnorm + lnorm[:1, :] - 2.0 * cross)
    return values


def at_anchors(value, picks):
    first = value.astype(BF16)
    rest = value - first.astype(F32)
    second = rest.astype(BF16)
    third = (rest - second.astype(F32)).astype(BF16)
    parts = jnp.concatenate([first, second, third], axis=0)
    parts = jnp.dot(parts, picks[...], preferred_element_type=F32)
    n = value.shape[0]
    return parts[:n] + parts[n : 2 * n] + parts[2 * n :]


def near_kernel(lags, *refs):
    pieces, (block, lnorm, picks, out, acc) = refs[:6], refs[6:]
    values = cross_rows(lags, pieces, block, lnorm, acc)
    out[...] = at_anchors(jnp.concatenate(values, axis=0), picks)


def away_kernel(lags, *refs):
    pieces, (block, lnorm, picks, near, out, acc) = refs[:6], refs[6:]
    values = cross_rows(lags, pieces, block, lnorm, acc)
    count = values[0].shape[0]
    value = at_anchors(jnp.concatenate(values, axis=0), picks)
    y, xh = place_on_y(), lax.axis_index("xh")
    for r, (dy, dx) in enumerate(NEAR + AWAY):
        owner = lax.rem(y + dy, 4) * 2 + lax.rem(xh + dx, 2)
        source, at = (near, r) if r < 4 else (value, r - 4)
        out[pl.ds(pl.multiple_of(owner * count, count), count), :] = source[at * count : (at + 1) * count, :]


def weights_kernel(dist, scale, picks, out):
    scores = -dist[...] / scale[:, :1]
    top = jnp.max(scores, axis=1, keepdims=True)
    top_hi, top_lo = halves(top)
    weights = jnp.exp(scores - (top_hi + top_lo)).astype(BF16)
    tot_hi, tot_lo = halves(jnp.sum(weights.astype(F32), axis=1, keepdims=True))
    wide = picks.shape[0]
    spread_out = lax.dot_general(weights, picks[...], (((1,), (1,)), ((), ())), preferred_element_type=F32)
    out[:, :wide] = spread_out.astype(BF16)
    out[:, wide:] = in_lanes((top_hi, top_lo, tot_hi, tot_lo)).astype(BF16)


def halves(value):
    first = value.astype(BF16).astype(F32)
    return first, (value - first).astype(BF16).astype(F32)


def in_lanes(columns):
    lane = lax.broadcasted_iota(jnp.int32, (columns[0].shape[0], 128), 1)
    value = columns[-1]
    for i in range(len(columns) - 2, -1, -1):
        value = jnp.where(lane == i, columns[i], value)
    return value


def mixing(leads, w, rows):
    targets, wide = w.shape[0], w.shape[1] - 128
    count = leads.shape[0]
    shape = (count * targets, count * targets)
    row, col = lax.broadcasted_iota(jnp.int32, shape, 0), lax.broadcasted_iota(jnp.int32, shape, 1)
    perm = jnp.where(lax.rem(row, count) * targets + lax.div(row, count) == col, 1.0, 0.0).astype(BF16)
    weights = w[:, :wide].astype(F32)
    stack = jnp.concatenate([pltpu.roll(weights, leads[k], 1) for k in range(count)], axis=0).astype(BF16)
    mixed = jnp.dot(perm, stack, preferred_element_type=F32).astype(BF16)[:, :rows]
    fact = jnp.concatenate([w[:, wide:]] * count, axis=0)
    return mixed, jnp.dot(perm, fact, preferred_element_type=F32)


def compose_own_kernel(leads, own, block, out, facts):
    rows = block.shape[0]
    quarter = out.shape[1] // 2
    mixed, facts[...] = mixing(leads, own, rows)
    odd = lax.axis_index("yl")
    for side, start in enumerate((2 * odd, 3 - 2 * odd)):
        mine = block[:, pl.ds(pl.multiple_of(start * quarter, quarter), quarter)]
        out[:, side * quarter : (side + 1) * quarter] = jnp.dot(mixed, mine, preferred_element_type=F32)


def compose_kernel(leads, partial, own_facts, up, down, block_up, block_down, out):
    rows, quarter = block_up.shape
    fact = own_facts[...]
    step = 512
    columns = []
    for side, (w, other) in enumerate(((up, block_up), (down, block_down))):
        mixed, there = mixing(leads, w, rows)
        tops = [f[:, 0:1] + f[:, 1:2] for f in (fact, there)]
        totals = [f[:, 2:3] + f[:, 3:4] for f in (fact, there)]
        larger = tops[0] >= tops[1]
        top = jnp.where(larger, tops[0], tops[1])
        first, second = jnp.exp(tops[0] - top), jnp.exp(tops[1] - top)
        columns += [jnp.where(larger, fact[:, j : j + 1], there[:, j : j + 1]) for j in range(2)]
        columns += halves(first * totals[0] + second * totals[1])
        for c in range(0, quarter, step):
            at = side * quarter + c
            value = second * jnp.dot(mixed, other[:, c : c + step], preferred_element_type=F32)
            out[:, at : at + step] = (value + first * partial[:, at : at + step]).astype(BF16)
    out[:, 2 * quarter :] = in_lanes(columns).astype(BF16)


def combine_kernel(parts, out):
    n, rows, wide = parts.shape
    count, lead_n, width = out.shape
    quarter = width // 4
    facts = [parts[b, :, wide - 128 :].astype(F32) for b in range(n)]
    step = 512
    for q in range(4):
        odd, side = ((0, 0), (1, 1), (1, 0), (0, 1))[q]
        sources = [b for b in range(n) if (b // 2) % 2 == odd]
        at = 4 * side
        tops = [facts[b][:, at : at + 1] + facts[b][:, at + 1 : at + 2] for b in sources]
        top = functools.reduce(jnp.maximum, tops)
        factors = [jnp.exp(t - top) for t in tops]
        total = sum(f * (facts[b][:, at + 2 : at + 3] + facts[b][:, at + 3 : at + 4]) for f, b in zip(factors, sources))
        factors = [f / total for f in factors]
        for c in range(0, quarter, step):
            from_c = side * quarter + c
            summed = sum(f * parts[b, :, from_c : from_c + step].astype(F32) for f, b in zip(factors, sources))
            summed = summed.reshape(count, lead_n, step).astype(BF16)
            out[:, :, q * quarter + c : q * quarter + c + step] = summed


def total_over_space(value, arriving):
    value = value + lax.ppermute(value, "co", flip(2, 1))
    both = [(z * 2 + x, (z ^ 1) * 2 + (x ^ 1)) for z in range(8) for x in range(2)]
    value = (value + lax.ppermute(value, ("z", "xl"), both)) + (lax.ppermute(value, "z", flip(8, 1)) + lax.ppermute(value, "xl", flip(2, 1)))
    value, arriving = lax.optimization_barrier((value, arriving))
    three = lax.ppermute(value, "z", [(z, (z - 3) % 8 if z % 2 == 0 else (z + 3) % 8) for z in range(8)])
    two = lax.ppermute(value, "z", [(z, (z - 2) % 8 if z % 2 == 0 else (z + 2) % 8) for z in range(8)])
    one = lax.ppermute(value, "z", [(z, (z - 1) % 8 if z % 2 == 0 else (z + 1) % 8) for z in range(8)])
    return value + one + two + three, arriving


def per_device(targets, library, anchors, leads, spread):
    lags, count, width = targets.shape
    rows = library.shape[0]
    lead_n = leads.shape[0]
    n_lib = lax.axis_size(LIB)
    n_target = count * n_lib
    wide = -(-rows // 128) * 128
    scale = math.sqrt(lags * width * lax.axis_size(SPACE))
    quarter = width // 4

    n_anchor = anchors.shape[0]
    ready = pl.pallas_call(
        functools.partial(prepare_kernel, lags, scale),
        out_shape=(
            jax.ShapeDtypeStruct((8, wide), F32),
            jax.ShapeDtypeStruct((wide, n_anchor), BF16),
            jax.ShapeDtypeStruct((n_target, 128), F32),
            jax.ShapeDtypeStruct((rows, quarter), BF16),
            jax.ShapeDtypeStruct((rows, quarter), BF16),
        ),
        in_specs=[VM] * 3,
        out_specs=(VM,) * 5,
        compiler_params=PARAMS,
        cost_estimate=pl.CostEstimate(flops=2 * rows * width, bytes_accessed=4 << 20, transcendentals=0),
        name="prepare",
    )(library, anchors.reshape(1, n_anchor), spread.reshape(1, n_target))
    near, away, ready = gather_targets(targets, ready)
    lnorm, picks, scales, for_up, for_down = ready

    flops = lags * n_target * wide * width
    near_dist = pl.pallas_call(
        functools.partial(near_kernel, lags),
        out_shape=jax.ShapeDtypeStruct((n_target // 2, n_anchor), F32),
        in_specs=[VM] * 9,
        out_specs=VM,
        scratch_shapes=[pltpu.VMEM((lags * n_target // 2, wide), F32)],
        compiler_params=PARAMS,
        cost_estimate=pl.CostEstimate(flops=flops, bytes_accessed=5 << 20, transcendentals=0),
        name="near",
    )(*near, library, lnorm, picks)

    for_up, for_down, near_dist = lax.optimization_barrier((for_up, for_down, near_dist))
    block_down = lax.ppermute(for_up, Y, turn(4, 1))
    block_up = lax.ppermute(for_down, Y, turn(4, -1))

    partial_dist = pl.pallas_call(
        functools.partial(away_kernel, lags),
        out_shape=jax.ShapeDtypeStruct((n_target, n_anchor), F32),
        in_specs=[VM] * 10,
        out_specs=VM,
        scratch_shapes=[pltpu.VMEM((lags * n_target // 2, wide), F32)],
        compiler_params=PARAMS,
        cost_estimate=pl.CostEstimate(flops=flops, bytes_accessed=5 << 20, transcendentals=0),
        name="away",
    )(*away, library, lnorm, picks, near_dist)

    dist, (block_up, block_down) = total_over_space(partial_dist, (block_up, block_down))
    own = pl.pallas_call(
        weights_kernel,
        out_shape=jax.ShapeDtypeStruct((n_target, wide + 128), BF16),
        in_specs=[VM] * 3,
        out_specs=VM,
        compiler_params=PARAMS,
        cost_estimate=pl.CostEstimate(flops=2 * n_target * wide * 256, bytes_accessed=1 << 20, transcendentals=n_target * 256),
        name="weights",
    )(dist, scales, picks)
    down = lax.ppermute(own, Y, turn(4, 1))
    up = lax.ppermute(own, Y, turn(4, -1))

    partial, facts = pl.pallas_call(
        compose_own_kernel,
        out_shape=(
            jax.ShapeDtypeStruct((lead_n * n_target, 2 * quarter), F32),
            jax.ShapeDtypeStruct((lead_n * n_target, 128), F32),
        ),
        in_specs=[SM] + [VM] * 2,
        out_specs=(VM,) * 2,
        compiler_params=PARAMS,
        cost_estimate=pl.CostEstimate(flops=lead_n * n_target * rows * width, bytes_accessed=5 << 20, transcendentals=0),
        name="compose_own",
    )(leads, own, library)
    parts = pl.pallas_call(
        compose_kernel,
        out_shape=jax.ShapeDtypeStruct((lead_n * n_target, 2 * quarter + 128), BF16),
        in_specs=[SM] + [VM] * 6,
        out_specs=VM,
        compiler_params=PARAMS,
        cost_estimate=pl.CostEstimate(flops=lead_n * n_target * rows * width, bytes_accessed=5 << 20, transcendentals=0),
        name="compose",
    )(leads, partial, facts, up, down, block_up, block_down)

    parts = parts.reshape(n_lib, lead_n * count, 2 * quarter + 128)
    parts = lax.all_to_all(parts, LIB, 0, 0, tiled=True)

    return pl.pallas_call(
        combine_kernel,
        out_shape=jax.ShapeDtypeStruct((count, lead_n, width), BF16),
        in_specs=[VM],
        out_specs=VM,
        compiler_params=PARAMS,
        cost_estimate=pl.CostEstimate(flops=2 * n_target * lead_n * width, bytes_accessed=3 << 20, transcendentals=0),
        name="combine",
    )(parts)


def solution(mesh):
    fine = Mesh(mesh.devices.reshape(8, 2, 2, 2, 2, 2), SPACE + LIB)
    placed = (P(None, LIB, SPACE), P(LIB, SPACE), P(LIB), P(), P())
    return jax.shard_map(per_device, mesh=fine, in_specs=placed, out_specs=P(LIB, None, SPACE), check_vma=False)
```

```python
import functools
import math

import jax
import jax.numpy as jnp
from jax import lax
from jax.experimental import pallas as pl
from jax.experimental.pallas import tpu as pltpu
from jax.sharding import Mesh, PartitionSpec as P

F32 = jnp.float32
BF16 = jnp.bfloat16
Y = ("yh", "yl")
LIB = ("yh", "yl", "xh")
SPACE = ("z", "xl", "co")
VM = pl.BlockSpec(memory_space=pltpu.VMEM)
SM = pl.BlockSpec(memory_space=pltpu.SMEM)
HB = pl.BlockSpec(memory_space=pltpu.HBM)
PARAMS = pltpu.CompilerParams(vmem_limit_bytes=16 * 1024 * 1024)
NEAR = ((0, 0), (0, 1), (3, 0), (1, 0))
AWAY = ((3, 1), (1, 1), (2, 0), (2, 1))


def flip(n, bit):
    return [(i, i ^ bit) for i in range(n)]


def turn(n, by):
    return [(i, (i + by) % n) for i in range(n)]


def gather_targets(targets, ready):
    lags, count, width = targets.shape
    own = targets.reshape(lags * count, width)
    half = lags * count // 2
    early, late = pl.pallas_call(
        split_kernel,
        out_shape=(jax.ShapeDtypeStruct((half, width), BF16),) * 2,
        in_specs=[HB],
        out_specs=(VM,) * 2,
        scratch_shapes=[pltpu.SemaphoreType.DMA((2,))],
        compiler_params=PARAMS,
        name="split",
    )(own)
    below_a = lax.ppermute(early, Y, turn(4, 1))
    above_b = lax.ppermute(late, Y, turn(4, -1))
    sent, early, late = lax.optimization_barrier((own, early, late))
    across = lax.ppermute(sent, "xh", flip(2, 1))
    below_b = lax.ppermute(late, Y, turn(4, 1))
    above_a = lax.ppermute(early, Y, turn(4, -1))
    below_a, above_b, ready = lax.optimization_barrier((below_a, above_b, ready))
    far_a = lax.ppermute(below_a, Y, turn(4, 1))
    far_b = lax.ppermute(above_b, Y, turn(4, -1))
    across, below_b, above_a = lax.optimization_barrier((across, below_b, above_a))
    below_x = lax.ppermute(across, Y, turn(4, 1))
    above_x = lax.ppermute(across, Y, turn(4, -1))
    far_xa = lax.ppermute(far_a, "xh", flip(2, 1))
    far_xb = lax.ppermute(far_b, "xh", flip(2, 1))
    return (own, across, below_a, below_b, above_a, above_b), (below_x, above_x, far_a, far_b, far_xa, far_xb), ready


def split_kernel(whole, early, late, sems):
    half = early.shape[0]
    first = pltpu.make_async_copy(whole.at[pl.ds(0, half), :], early, sems.at[0])
    second = pltpu.make_async_copy(whole.at[pl.ds(half, half), :], late, sems.at[1])
    first.start()
    second.start()
    first.wait()
    second.wait()


def place_on_y():
    return lax.axis_index("yh") * 2 + lax.axis_index("yl")


def prepare_kernel(lags, factor, library, anchors, spread, lnorm, picks, scale, for_up, for_down):
    rows, width = library.shape
    wide = picks.shape[0]
    squares = jnp.zeros((rows, 128), F32)
    for c in range(0, width, 128):
        part = library[:, c : c + 128].astype(F32)
        squares = squares + part * part
    squares = jnp.concatenate([squares, jnp.zeros((wide - rows, 128), F32)], axis=0)
    norm = jnp.sum(squares.T, axis=0, keepdims=True)
    norm = jnp.broadcast_to(norm, lnorm.shape)
    total = norm
    for lag in range(1, lags):
        total = total + pltpu.roll(norm, lag, 1)
    lnorm[...] = total
    spots = lax.broadcasted_iota(jnp.int32, picks.shape, 0)
    picks[...] = jnp.where(spots == anchors[...], 1.0, 0.0).astype(BF16)
    count = scale.shape[0]
    wider = jnp.concatenate([spread[...] * factor, jnp.ones((1, 128 - count), F32)], axis=1)
    scale[...] = jnp.broadcast_to(wider, (128, 128)).T[:count, :]
    quarter = for_up.shape[1]
    odd = lax.axis_index("yl")
    for_up[...] = library[:, pl.ds(pl.multiple_of((1 + 2 * odd) * quarter, quarter), quarter)]
    for_down[...] = library[:, pl.ds(pl.multiple_of((2 - 2 * odd) * quarter, quarter), quarter)]


def cross_rows(lags, pieces, block, lnorm, acc):
    rows, width = block.shape
    acc[...] = jnp.zeros_like(acc)
    lhs = jnp.concatenate([p[...] for p in pieces], axis=0)
    acc[:, :rows] = lax.dot_general(lhs, block[...], (((1,), (1,)), ((), ())), preferred_element_type=F32)
    norms = jnp.zeros((acc.shape[0], 128), F32)
    for c in range(0, width, 128):
        part = lhs[:, c : c + 128].astype(F32)
        norms = norms + part * part
    norms = jnp.sum(norms, axis=1, keepdims=True)
    count = acc.shape[0] // 4 // lags
    values = []
    for r in range(4):
        cross = jnp.zeros((count, acc.shape[1]), F32)
        tnorm = jnp.zeros((count, 1), F32)
        for lag in range(lags):
            at = (r * lags + lag) * count
            here = acc[at : at + count, :]
            cross = cross + (pltpu.roll(here, lag, 1) if lag else here)
            tnorm = tnorm + norms[at : at + count]
        values.append(tnorm + lnorm[:1, :] - 2.0 * cross)
    return values


def at_anchors(value, picks):
    first = value.astype(BF16)
    rest = value - first.astype(F32)
    second = rest.astype(BF16)
    third = (rest - second.astype(F32)).astype(BF16)
    parts = jnp.concatenate([first, second, third], axis=0)
    parts = jnp.dot(parts, picks[...], preferred_element_type=F32)
    n = value.shape[0]
    return parts[:n] + parts[n : 2 * n] + parts[2 * n :]


def near_kernel(lags, *refs):
    pieces, (block, lnorm, picks, out, acc) = refs[:6], refs[6:]
    values = cross_rows(lags, pieces, block, lnorm, acc)
    out[...] = at_anchors(jnp.concatenate(values, axis=0), picks)


def away_kernel(lags, *refs):
    pieces, (block, lnorm, picks, near, out, acc) = refs[:6], refs[6:]
    values = cross_rows(lags, pieces, block, lnorm, acc)
    count = values[0].shape[0]
    value = at_anchors(jnp.concatenate(values, axis=0), picks)
    y, xh = place_on_y(), lax.axis_index("xh")
    for r, (dy, dx) in enumerate(NEAR + AWAY):
        owner = lax.rem(y + dy, 4) * 2 + lax.rem(xh + dx, 2)
        source, at = (near, r) if r < 4 else (value, r - 4)
        out[pl.ds(pl.multiple_of(owner * count, count), count), :] = source[at * count : (at + 1) * count, :]


def weights_kernel(dist, scale, picks, out):
    scores = -dist[...] / scale[:, :1]
    top = jnp.max(scores, axis=1, keepdims=True)
    top_hi, top_lo = halves(top)
    weights = jnp.exp(scores - (top_hi + top_lo)).astype(BF16)
    tot_hi, tot_lo = halves(jnp.sum(weights.astype(F32), axis=1, keepdims=True))
    wide = picks.shape[0]
    spread_out = lax.dot_general(weights, picks[...], (((1,), (1,)), ((), ())), preferred_element_type=F32)
    out[:, :wide] = spread_out.astype(BF16)
    out[:, wide:] = in_lanes((top_hi, top_lo, tot_hi, tot_lo)).astype(BF16)


def halves(value):
    first = value.astype(BF16).astype(F32)
    return first, (value - first).astype(BF16).astype(F32)


def in_lanes(columns):
    lane = lax.broadcasted_iota(jnp.int32, (columns[0].shape[0], 128), 1)
    value = columns[-1]
    for i in range(len(columns) - 2, -1, -1):
        value = jnp.where(lane == i, columns[i], value)
    return value


def mixing(leads, w, rows):
    targets, wide = w.shape[0], w.shape[1] - 128
    count = leads.shape[0]
    shape = (count * targets, count * targets)
    row, col = lax.broadcasted_iota(jnp.int32, shape, 0), lax.broadcasted_iota(jnp.int32, shape, 1)
    perm = jnp.where(lax.rem(row, count) * targets + lax.div(row, count) == col, 1.0, 0.0).astype(BF16)
    weights = w[:, :wide].astype(F32)
    stack = jnp.concatenate([pltpu.roll(weights, leads[k], 1) for k in range(count)], axis=0).astype(BF16)
    mixed = jnp.dot(perm, stack, preferred_element_type=F32).astype(BF16)[:, :rows]
    fact = jnp.concatenate([w[:, wide:]] * count, axis=0)
    return mixed, jnp.dot(perm, fact, preferred_element_type=F32)


def compose_own_kernel(leads, own, block, out, facts):
    rows = block.shape[0]
    quarter = out.shape[1] // 2
    mixed, facts[...] = mixing(leads, own, rows)
    odd = lax.axis_index("yl")
    for side, start in enumerate((2 * odd, 3 - 2 * odd)):
        mine = block[:, pl.ds(pl.multiple_of(start * quarter, quarter), quarter)]
        out[:, side * quarter : (side + 1) * quarter] = jnp.dot(mixed, mine, preferred_element_type=F32)


def compose_kernel(leads, partial, own_facts, up, down, block_up, block_down, out):
    rows, quarter = block_up.shape
    fact = own_facts[...]
    step = 512
    columns = []
    for side, (w, other) in enumerate(((up, block_up), (down, block_down))):
        mixed, there = mixing(leads, w, rows)
        tops = [f[:, 0:1] + f[:, 1:2] for f in (fact, there)]
        totals = [f[:, 2:3] + f[:, 3:4] for f in (fact, there)]
        larger = tops[0] >= tops[1]
        top = jnp.where(larger, tops[0], tops[1])
        first, second = jnp.exp(tops[0] - top), jnp.exp(tops[1] - top)
        columns += [jnp.where(larger, fact[:, j : j + 1], there[:, j : j + 1]) for j in range(2)]
        columns += halves(first * totals[0] + second * totals[1])
        for c in range(0, quarter, step):
            at = side * quarter + c
            value = second * jnp.dot(mixed, other[:, c : c + step], preferred_element_type=F32)
            out[:, at : at + step] = (value + first * partial[:, at : at + step]).astype(BF16)
    out[:, 2 * quarter :] = in_lanes(columns).astype(BF16)


def combine_kernel(parts, out):
    n, rows, wide = parts.shape
    count, lead_n, width = out.shape
    quarter = width // 4
    facts = [parts[b, :, wide - 128 :].astype(F32) for b in range(n)]
    step = 512
    for q in range(4):
        odd, side = ((0, 0), (1, 1), (1, 0), (0, 1))[q]
        sources = [b for b in range(n) if (b // 2) % 2 == odd]
        at = 4 * side
        tops = [facts[b][:, at : at + 1] + facts[b][:, at + 1 : at + 2] for b in sources]
        top = functools.reduce(jnp.maximum, tops)
        factors = [jnp.exp(t - top) for t in tops]
        total = sum(f * (facts[b][:, at + 2 : at + 3] + facts[b][:, at + 3 : at + 4]) for f, b in zip(factors, sources))
        factors = [f / total for f in factors]
        for c in range(0, quarter, step):
            from_c = side * quarter + c
            summed = sum(f * parts[b, :, from_c : from_c + step].astype(F32) for f, b in zip(factors, sources))
            summed = summed.reshape(count, lead_n, step).astype(BF16)
            out[:, :, q * quarter + c : q * quarter + c + step] = summed


def total_over_space(value, arriving):
    value = value + lax.ppermute(value, "co", flip(2, 1))
    both = [(z * 2 + x, (z ^ 1) * 2 + (x ^ 1)) for z in range(8) for x in range(2)]
    value = (value + lax.ppermute(value, "xl", flip(2, 1))) + (lax.ppermute(value, "z", flip(8, 1)) + lax.ppermute(value, ("z", "xl"), both))
    three = lax.ppermute(value, "z", [(z, (z - 3) % 8 if z % 2 == 0 else (z + 3) % 8) for z in range(8)])
    two = lax.ppermute(value, "z", [(z, (z - 2) % 8 if z % 2 == 0 else (z + 2) % 8) for z in range(8)])
    last, arriving = lax.optimization_barrier((value, arriving))
    one = lax.ppermute(last, "z", [(z, (z - 1) % 8 if z % 2 == 0 else (z + 1) % 8) for z in range(8)])
    return value + one + two + three, arriving


def per_device(targets, library, anchors, leads, spread):
    lags, count, width = targets.shape
    rows = library.shape[0]
    lead_n = leads.shape[0]
    n_lib = lax.axis_size(LIB)
    n_target = count * n_lib
    wide = -(-rows // 128) * 128
    scale = math.sqrt(lags * width * lax.axis_size(SPACE))
    quarter = width // 4

    n_anchor = anchors.shape[0]
    ready = pl.pallas_call(
        functools.partial(prepare_kernel, lags, scale),
        out_shape=(
            jax.ShapeDtypeStruct((8, wide), F32),
            jax.ShapeDtypeStruct((wide, n_anchor), BF16),
            jax.ShapeDtypeStruct((n_target, 128), F32),
            jax.ShapeDtypeStruct((rows, quarter), BF16),
            jax.ShapeDtypeStruct((rows, quarter), BF16),
        ),
        in_specs=[VM] * 3,
        out_specs=(VM,) * 5,
        compiler_params=PARAMS,
        cost_estimate=pl.CostEstimate(flops=2 * rows * width, bytes_accessed=4 << 20, transcendentals=0),
        name="prepare",
    )(library, anchors.reshape(1, n_anchor), spread.reshape(1, n_target))
    near, away, ready = gather_targets(targets, ready)
    lnorm, picks, scales, for_up, for_down = ready

    flops = lags * n_target * wide * width
    near_dist = pl.pallas_call(
        functools.partial(near_kernel, lags),
        out_shape=jax.ShapeDtypeStruct((n_target // 2, n_anchor), F32),
        in_specs=[VM] * 9,
        out_specs=VM,
        scratch_shapes=[pltpu.VMEM((lags * n_target // 2, wide), F32)],
        compiler_params=PARAMS,
        cost_estimate=pl.CostEstimate(flops=flops, bytes_accessed=5 << 20, transcendentals=0),
        name="near",
    )(*near, library, lnorm, picks)

    for_up, for_down, near_dist = lax.optimization_barrier((for_up, for_down, near_dist))
    block_down = lax.ppermute(for_up, Y, turn(4, 1))
    block_up = lax.ppermute(for_down, Y, turn(4, -1))

    partial_dist = pl.pallas_call(
        functools.partial(away_kernel, lags),
        out_shape=jax.ShapeDtypeStruct((n_target, n_anchor), F32),
        in_specs=[VM] * 10,
        out_specs=VM,
        scratch_shapes=[pltpu.VMEM((lags * n_target // 2, wide), F32)],
        compiler_params=PARAMS,
        cost_estimate=pl.CostEstimate(flops=flops, bytes_accessed=5 << 20, transcendentals=0),
        name="away",
    )(*away, library, lnorm, picks, near_dist)

    dist, (block_up, block_down) = total_over_space(partial_dist, (block_up, block_down))
    own = pl.pallas_call(
        weights_kernel,
        out_shape=jax.ShapeDtypeStruct((n_target, wide + 128), BF16),
        in_specs=[VM] * 3,
        out_specs=VM,
        compiler_params=PARAMS,
        cost_estimate=pl.CostEstimate(flops=2 * n_target * wide * 256, bytes_accessed=1 << 20, transcendentals=n_target * 256),
        name="weights",
    )(dist, scales, picks)
    down = lax.ppermute(own, Y, turn(4, 1))
    up = lax.ppermute(own, Y, turn(4, -1))

    partial, facts = pl.pallas_call(
        compose_own_kernel,
        out_shape=(
            jax.ShapeDtypeStruct((lead_n * n_target, 2 * quarter), F32),
            jax.ShapeDtypeStruct((lead_n * n_target, 128), F32),
        ),
        in_specs=[SM] + [VM] * 2,
        out_specs=(VM,) * 2,
        compiler_params=PARAMS,
        cost_estimate=pl.CostEstimate(flops=lead_n * n_target * rows * width, bytes_accessed=5 << 20, transcendentals=0),
        name="compose_own",
    )(leads, own, library)
    parts = pl.pallas_call(
        compose_kernel,
        out_shape=jax.ShapeDtypeStruct((lead_n * n_target, 2 * quarter + 128), BF16),
        in_specs=[SM] + [VM] * 6,
        out_specs=VM,
        compiler_params=PARAMS,
        cost_estimate=pl.CostEstimate(flops=lead_n * n_target * rows * width, bytes_accessed=5 << 20, transcendentals=0),
        name="compose",
    )(leads, partial, facts, up, down, block_up, block_down)

    parts = parts.reshape(n_lib, lead_n * count, 2 * quarter + 128)
    parts = lax.all_to_all(parts, LIB, 0, 0, tiled=True)

    return pl.pallas_call(
        combine_kernel,
        out_shape=jax.ShapeDtypeStruct((count, lead_n, width), BF16),
        in_specs=[VM],
        out_specs=VM,
        compiler_params=PARAMS,
        cost_estimate=pl.CostEstimate(flops=2 * n_target * lead_n * width, bytes_accessed=3 << 20, transcendentals=0),
        name="combine",
    )(parts)


def solution(mesh):
    fine = Mesh(mesh.devices.reshape(8, 2, 2, 2, 2, 2), SPACE + LIB)
    placed = (P(None, LIB, SPACE), P(LIB, SPACE), P(LIB), P(), P())
    return jax.shard_map(per_device, mesh=fine, in_specs=placed, out_specs=P(LIB, None, SPACE), check_vma=False)
```

```python
import functools
import math

import jax
import jax.numpy as jnp
from jax import lax
from jax.experimental import pallas as pl
from jax.experimental.pallas import tpu as pltpu
from jax.sharding import Mesh, PartitionSpec as P

F32 = jnp.float32
BF16 = jnp.bfloat16
Y = ("yh", "yl")
LIB = ("yh", "yl", "xh")
SPACE = ("z", "xl", "co")
VM = pl.BlockSpec(memory_space=pltpu.VMEM)
SM = pl.BlockSpec(memory_space=pltpu.SMEM)
HB = pl.BlockSpec(memory_space=pltpu.HBM)
ANY = pl.BlockSpec(memory_space=pl.ANY)
PARAMS = pltpu.CompilerParams(vmem_limit_bytes=16 * 1024 * 1024)
NEAR = ((0, 0), (0, 1), (3, 0), (1, 0))
AWAY = ((3, 1), (1, 1), (2, 0), (2, 1))


def flip(n, bit):
    return [(i, i ^ bit) for i in range(n)]


def turn(n, by):
    return [(i, (i + by) % n) for i in range(n)]


def gather_targets(targets, ready):
    lags, count, width = targets.shape
    own = targets.reshape(lags * count, width)
    half = lags * count // 2
    early, late = pl.pallas_call(
        split_kernel,
        out_shape=(jax.ShapeDtypeStruct((half, width), BF16),) * 2,
        in_specs=[HB],
        out_specs=(VM,) * 2,
        scratch_shapes=[pltpu.SemaphoreType.DMA((2,))],
        compiler_params=PARAMS,
        name="split",
    )(own)
    below_a = lax.ppermute(early, Y, turn(4, 1))
    above_b = lax.ppermute(late, Y, turn(4, -1))
    sent, early, late = lax.optimization_barrier((own, early, late))
    across = lax.ppermute(sent, "xh", flip(2, 1))
    below_b = lax.ppermute(late, Y, turn(4, 1))
    above_a = lax.ppermute(early, Y, turn(4, -1))
    below_a, above_b, ready = lax.optimization_barrier((below_a, above_b, ready))
    below_a, above_b = pl.pallas_call(
        stay_kernel,
        out_shape=(jax.ShapeDtypeStruct(below_a.shape, BF16),) * 2,
        in_specs=[ANY] * 2,
        out_specs=(ANY,) * 2,
        input_output_aliases={0: 0, 1: 1},
        compiler_params=PARAMS,
        cost_estimate=pl.CostEstimate(flops=1 << 30, bytes_accessed=1 << 20, transcendentals=0),
        name="stay",
    )(below_a, above_b)
    far_a = lax.ppermute(below_a, Y, turn(4, 1))
    far_b = lax.ppermute(above_b, Y, turn(4, -1))
    across, below_b, above_a = lax.optimization_barrier((across, below_b, above_a))
    below_x = lax.ppermute(across, Y, turn(4, 1))
    above_x = lax.ppermute(across, Y, turn(4, -1))
    far_xa = lax.ppermute(far_a, "xh", flip(2, 1))
    far_xb = lax.ppermute(far_b, "xh", flip(2, 1))
    return (own, across, below_a, below_b, above_a, above_b), (below_x, above_x, far_a, far_b, far_xa, far_xb), ready


def stay_kernel(*refs):
    pass


def split_kernel(whole, early, late, sems):
    half = early.shape[0]
    first = pltpu.make_async_copy(whole.at[pl.ds(0, half), :], early, sems.at[0])
    second = pltpu.make_async_copy(whole.at[pl.ds(half, half), :], late, sems.at[1])
    first.start()
    second.start()
    first.wait()
    second.wait()


def place_on_y():
    return lax.axis_index("yh") * 2 + lax.axis_index("yl")


def prepare_kernel(lags, factor, library, anchors, spread, lnorm, picks, scale, for_up, for_down):
    rows, width = library.shape
    wide = picks.shape[0]
    squares = jnp.zeros((rows, 128), F32)
    for c in range(0, width, 128):
        part = library[:, c : c + 128].astype(F32)
        squares = squares + part * part
    squares = jnp.concatenate([squares, jnp.zeros((wide - rows, 128), F32)], axis=0)
    norm = jnp.sum(squares.T, axis=0, keepdims=True)
    norm = jnp.broadcast_to(norm, lnorm.shape)
    total = norm
    for lag in range(1, lags):
        total = total + pltpu.roll(norm, lag, 1)
    lnorm[...] = total
    spots = lax.broadcasted_iota(jnp.int32, picks.shape, 0)
    picks[...] = jnp.where(spots == anchors[...], 1.0, 0.0).astype(BF16)
    count = scale.shape[0]
    wider = jnp.concatenate([spread[...] * factor, jnp.ones((1, 128 - count), F32)], axis=1)
    scale[...] = jnp.broadcast_to(wider, (128, 128)).T[:count, :]
    quarter = for_up.shape[1]
    odd = lax.axis_index("yl")
    for_up[...] = library[:, pl.ds(pl.multiple_of((1 + 2 * odd) * quarter, quarter), quarter)]
    for_down[...] = library[:, pl.ds(pl.multiple_of((2 - 2 * odd) * quarter, quarter), quarter)]


def cross_rows(lags, pieces, block, lnorm, acc):
    rows, width = block.shape
    acc[...] = jnp.zeros_like(acc)
    lhs = jnp.concatenate([p[...] for p in pieces], axis=0)
    acc[:, :rows] = lax.dot_general(lhs, block[...], (((1,), (1,)), ((), ())), preferred_element_type=F32)
    norms = jnp.zeros((acc.shape[0], 128), F32)
    for c in range(0, width, 128):
        part = lhs[:, c : c + 128].astype(F32)
        norms = norms + part * part
    norms = jnp.sum(norms, axis=1, keepdims=True)
    count = acc.shape[0] // 4 // lags
    values = []
    for r in range(4):
        cross = jnp.zeros((count, acc.shape[1]), F32)
        tnorm = jnp.zeros((count, 1), F32)
        for lag in range(lags):
            at = (r * lags + lag) * count
            here = acc[at : at + count, :]
            cross = cross + (pltpu.roll(here, lag, 1) if lag else here)
            tnorm = tnorm + norms[at : at + count]
        values.append(tnorm + lnorm[:1, :] - 2.0 * cross)
    return values


def at_anchors(value, picks):
    first = value.astype(BF16)
    rest = value - first.astype(F32)
    second = rest.astype(BF16)
    third = (rest - second.astype(F32)).astype(BF16)
    parts = jnp.concatenate([first, second, third], axis=0)
    parts = jnp.dot(parts, picks[...], preferred_element_type=F32)
    n = value.shape[0]
    return parts[:n] + parts[n : 2 * n] + parts[2 * n :]


def near_kernel(lags, *refs):
    pieces, (block, lnorm, picks, out, acc) = refs[:6], refs[6:]
    values = cross_rows(lags, pieces, block, lnorm, acc)
    out[...] = at_anchors(jnp.concatenate(values, axis=0), picks)


def away_kernel(lags, *refs):
    pieces, (block, lnorm, picks, near, out, acc) = refs[:6], refs[6:]
    values = cross_rows(lags, pieces, block, lnorm, acc)
    count = values[0].shape[0]
    value = at_anchors(jnp.concatenate(values, axis=0), picks)
    y, xh = place_on_y(), lax.axis_index("xh")
    for r, (dy, dx) in enumerate(NEAR + AWAY):
        owner = lax.rem(y + dy, 4) * 2 + lax.rem(xh + dx, 2)
        source, at = (near, r) if r < 4 else (value, r - 4)
        out[pl.ds(pl.multiple_of(owner * count, count), count), :] = source[at * count : (at + 1) * count, :]


def weights_kernel(dist, scale, picks, out):
    scores = -dist[...] / scale[:, :1]
    top = jnp.max(scores, axis=1, keepdims=True)
    top_hi, top_lo = halves(top)
    weights = jnp.exp(scores - (top_hi + top_lo)).astype(BF16)
    tot_hi, tot_lo = halves(jnp.sum(weights.astype(F32), axis=1, keepdims=True))
    wide = picks.shape[0]
    spread_out = lax.dot_general(weights, picks[...], (((1,), (1,)), ((), ())), preferred_element_type=F32)
    out[:, :wide] = spread_out.astype(BF16)
    out[:, wide:] = in_lanes((top_hi, top_lo, tot_hi, tot_lo)).astype(BF16)


def halves(value):
    first = value.astype(BF16).astype(F32)
    return first, (value - first).astype(BF16).astype(F32)


def in_lanes(columns):
    lane = lax.broadcasted_iota(jnp.int32, (columns[0].shape[0], 128), 1)
    value = columns[-1]
    for i in range(len(columns) - 2, -1, -1):
        value = jnp.where(lane == i, columns[i], value)
    return value


def by_target(shape, count):
    row, col = lax.broadcasted_iota(jnp.int32, shape, 0), lax.broadcasted_iota(jnp.int32, shape, 1)
    targets = shape[0] // count
    return jnp.where(lax.rem(row, count) * targets + lax.div(row, count) == col, 1.0, 0.0).astype(BF16)


def mixing(leads, w, perm, rows):
    wide = w.shape[1] - 128
    count = leads.shape[0]
    weights = w[:, :wide].astype(F32)
    stack = jnp.concatenate([pltpu.roll(weights, leads[k], 1) for k in range(count)], axis=0).astype(BF16)
    mixed = jnp.dot(perm, stack, preferred_element_type=F32).astype(BF16)[:, :rows]
    fact = jnp.concatenate([w[:, wide:]] * count, axis=0)
    return mixed, jnp.dot(perm, fact, preferred_element_type=F32)


def compose_own_kernel(leads, own, block, out, facts, order):
    rows = block.shape[0]
    quarter = out.shape[1] // 2
    perm = by_target(order.shape, leads.shape[0])
    order[...] = perm
    mixed, facts[...] = mixing(leads, own, perm, rows)
    odd = lax.axis_index("yl")
    for side, start in enumerate((2 * odd, 3 - 2 * odd)):
        mine = block[:, pl.ds(pl.multiple_of(start * quarter, quarter), quarter)]
        out[:, side * quarter : (side + 1) * quarter] = jnp.dot(mixed, mine, preferred_element_type=F32)


def compose_kernel(leads, partial, own_facts, order, up, down, block_up, block_down, out):
    rows, quarter = block_up.shape
    fact = own_facts[...]
    perm = order[...]
    step = 512
    columns = []
    for side, (w, other) in enumerate(((up, block_up), (down, block_down))):
        mixed, there = mixing(leads, w, perm, rows)
        tops = [f[:, 0:1] + f[:, 1:2] for f in (fact, there)]
        totals = [f[:, 2:3] + f[:, 3:4] for f in (fact, there)]
        larger = tops[0] >= tops[1]
        top = jnp.where(larger, tops[0], tops[1])
        first, second = jnp.exp(tops[0] - top), jnp.exp(tops[1] - top)
        columns += [jnp.where(larger, fact[:, j : j + 1], there[:, j : j + 1]) for j in range(2)]
        columns += halves(first * totals[0] + second * totals[1])
        for c in range(0, quarter, step):
            at = side * quarter + c
            value = second * jnp.dot(mixed, other[:, c : c + step], preferred_element_type=F32)
            out[:, at : at + step] = (value + first * partial[:, at : at + step]).astype(BF16)
    out[:, 2 * quarter :] = in_lanes(columns).astype(BF16)


def combine_kernel(parts, out):
    n, rows, wide = parts.shape
    count, lead_n, width = out.shape
    quarter = width // 4
    facts = [parts[b, :, wide - 128 :].astype(F32) for b in range(n)]
    step = 512
    for q in range(4):
        odd, side = ((0, 0), (1, 1), (1, 0), (0, 1))[q]
        sources = [b for b in range(n) if (b // 2) % 2 == odd]
        at = 4 * side
        tops = [facts[b][:, at : at + 1] + facts[b][:, at + 1 : at + 2] for b in sources]
        top = functools.reduce(jnp.maximum, tops)
        factors = [jnp.exp(t - top) for t in tops]
        total = sum(f * (facts[b][:, at + 2 : at + 3] + facts[b][:, at + 3 : at + 4]) for f, b in zip(factors, sources))
        factors = [f / total for f in factors]
        for c in range(0, quarter, step):
            from_c = side * quarter + c
            summed = sum(f * parts[b, :, from_c : from_c + step].astype(F32) for f, b in zip(factors, sources))
            summed = summed.reshape(count, lead_n, step).astype(BF16)
            out[:, :, q * quarter + c : q * quarter + c + step] = summed


def total_over_space(value, arriving):
    value = value + lax.ppermute(value, "co", flip(2, 1))
    both = [(z * 2 + x, (z ^ 1) * 2 + (x ^ 1)) for z in range(8) for x in range(2)]
    value = (value + lax.ppermute(value, "xl", flip(2, 1))) + (lax.ppermute(value, "z", flip(8, 1)) + lax.ppermute(value, ("z", "xl"), both))
    three = lax.ppermute(value, "z", [(z, (z - 3) % 8 if z % 2 == 0 else (z + 3) % 8) for z in range(8)])
    two = lax.ppermute(value, "z", [(z, (z - 2) % 8 if z % 2 == 0 else (z + 2) % 8) for z in range(8)])
    last, arriving = lax.optimization_barrier((value, arriving))
    one = lax.ppermute(last, "z", [(z, (z - 1) % 8 if z % 2 == 0 else (z + 1) % 8) for z in range(8)])
    return value + one + two + three, arriving


def per_device(targets, library, anchors, leads, spread):
    lags, count, width = targets.shape
    rows = library.shape[0]
    lead_n = leads.shape[0]
    n_lib = lax.axis_size(LIB)
    n_target = count * n_lib
    wide = -(-rows // 128) * 128
    scale = math.sqrt(lags * width * lax.axis_size(SPACE))
    quarter = width // 4

    n_anchor = anchors.shape[0]
    ready = pl.pallas_call(
        functools.partial(prepare_kernel, lags, scale),
        out_shape=(
            jax.ShapeDtypeStruct((8, wide), F32),
            jax.ShapeDtypeStruct((wide, n_anchor), BF16),
            jax.ShapeDtypeStruct((n_target, 128), F32),
            jax.ShapeDtypeStruct((rows, quarter), BF16),
            jax.ShapeDtypeStruct((rows, quarter), BF16),
        ),
        in_specs=[VM] * 3,
        out_specs=(VM,) * 5,
        compiler_params=PARAMS,
        cost_estimate=pl.CostEstimate(flops=2 * rows * width, bytes_accessed=4 << 20, transcendentals=0),
        name="prepare",
    )(library, anchors.reshape(1, n_anchor), spread.reshape(1, n_target))
    near, away, ready = gather_targets(targets, ready)
    lnorm, picks, scales, for_up, for_down = ready

    flops = lags * n_target * wide * width
    near_dist = pl.pallas_call(
        functools.partial(near_kernel, lags),
        out_shape=jax.ShapeDtypeStruct((n_target // 2, n_anchor), F32),
        in_specs=[VM] * 9,
        out_specs=VM,
        scratch_shapes=[pltpu.VMEM((lags * n_target // 2, wide), F32)],
        compiler_params=PARAMS,
        cost_estimate=pl.CostEstimate(flops=flops, bytes_accessed=5 << 20, transcendentals=0),
        name="near",
    )(*near, library, lnorm, picks)

    for_up, for_down, near_dist = lax.optimization_barrier((for_up, for_down, near_dist))
    block_down = lax.ppermute(for_up, Y, turn(4, 1))
    block_up = lax.ppermute(for_down, Y, turn(4, -1))

    partial_dist = pl.pallas_call(
        functools.partial(away_kernel, lags),
        out_shape=jax.ShapeDtypeStruct((n_target, n_anchor), F32),
        in_specs=[VM] * 10,
        out_specs=VM,
        scratch_shapes=[pltpu.VMEM((lags * n_target // 2, wide), F32)],
        compiler_params=PARAMS,
        cost_estimate=pl.CostEstimate(flops=flops, bytes_accessed=5 << 20, transcendentals=0),
        name="away",
    )(*away, library, lnorm, picks, near_dist)

    dist, (block_up, block_down) = total_over_space(partial_dist, (block_up, block_down))
    own = pl.pallas_call(
        weights_kernel,
        out_shape=jax.ShapeDtypeStruct((n_target, wide + 128), BF16),
        in_specs=[VM] * 3,
        out_specs=VM,
        compiler_params=PARAMS,
        cost_estimate=pl.CostEstimate(flops=2 * n_target * wide * 256, bytes_accessed=1 << 20, transcendentals=n_target * 256),
        name="weights",
    )(dist, scales, picks)
    down = lax.ppermute(own, Y, turn(4, 1))
    up = lax.ppermute(own, Y, turn(4, -1))

    partial, facts, order = pl.pallas_call(
        compose_own_kernel,
        out_shape=(
            jax.ShapeDtypeStruct((lead_n * n_target, 2 * quarter), F32),
            jax.ShapeDtypeStruct((lead_n * n_target, 128), F32),
            jax.ShapeDtypeStruct((lead_n * n_target, lead_n * n_target), BF16),
        ),
        in_specs=[SM] + [VM] * 2,
        out_specs=(VM,) * 3,
        compiler_params=PARAMS,
        cost_estimate=pl.CostEstimate(flops=lead_n * n_target * rows * width, bytes_accessed=5 << 20, transcendentals=0),
        name="compose_own",
    )(leads, own, library)
    parts = pl.pallas_call(
        compose_kernel,
        out_shape=jax.ShapeDtypeStruct((lead_n * n_target, 2 * quarter + 128), BF16),
        in_specs=[SM] + [VM] * 7,
        out_specs=VM,
        compiler_params=PARAMS,
        cost_estimate=pl.CostEstimate(flops=lead_n * n_target * rows * width, bytes_accessed=5 << 20, transcendentals=0),
        name="compose",
    )(leads, partial, facts, order, up, down, block_up, block_down)

    parts = parts.reshape(n_lib, lead_n * count, 2 * quarter + 128)
    parts = lax.all_to_all(parts, LIB, 0, 0, tiled=True)

    return pl.pallas_call(
        combine_kernel,
        out_shape=jax.ShapeDtypeStruct((count, lead_n, width), BF16),
        in_specs=[VM],
        out_specs=VM,
        compiler_params=PARAMS,
        cost_estimate=pl.CostEstimate(flops=2 * n_target * lead_n * width, bytes_accessed=3 << 20, transcendentals=0),
        name="combine",
    )(parts)


def solution(mesh):
    fine = Mesh(mesh.devices.reshape(8, 2, 2, 2, 2, 2), SPACE + LIB)
    placed = (P(None, LIB, SPACE), P(LIB, SPACE), P(LIB), P(), P())
    return jax.shard_map(per_device, mesh=fine, in_specs=placed, out_specs=P(LIB, None, SPACE), check_vma=False)
```

```python
import functools
import math

import jax
import jax.numpy as jnp
from jax import lax
from jax.experimental import pallas as pl
from jax.experimental.pallas import tpu as pltpu
from jax.sharding import Mesh, PartitionSpec as P

F32 = jnp.float32
BF16 = jnp.bfloat16
Y = ("yh", "yl")
LIB = ("yh", "yl", "xh")
SPACE = ("z", "xl", "co")
VM = pl.BlockSpec(memory_space=pltpu.VMEM)
SM = pl.BlockSpec(memory_space=pltpu.SMEM)
HB = pl.BlockSpec(memory_space=pltpu.HBM)
ANY = pl.BlockSpec(memory_space=pl.ANY)
PARAMS = pltpu.CompilerParams(vmem_limit_bytes=16 * 1024 * 1024)
NEAR = ((0, 0), (0, 1), (3, 0), (1, 0))
AWAY = ((3, 1), (1, 1), (2, 0), (2, 1))


def flip(n, bit):
    return [(i, i ^ bit) for i in range(n)]


def turn(n, by):
    return [(i, (i + by) % n) for i in range(n)]


def gather_targets(targets, ready):
    lags, count, width = targets.shape
    own = targets.reshape(lags * count, width)
    half = lags * count // 2
    early, late = pl.pallas_call(
        split_kernel,
        out_shape=(jax.ShapeDtypeStruct((half, width), BF16),) * 2,
        in_specs=[HB],
        out_specs=(VM,) * 2,
        scratch_shapes=[pltpu.SemaphoreType.DMA((2,))],
        compiler_params=PARAMS,
        name="split",
    )(own)
    below_a = lax.ppermute(early, Y, turn(4, 1))
    above_b = lax.ppermute(late, Y, turn(4, -1))
    sent, early, late = lax.optimization_barrier((own, early, late))
    across = lax.ppermute(sent, "xh", flip(2, 1))
    below_b = lax.ppermute(late, Y, turn(4, 1))
    above_a = lax.ppermute(early, Y, turn(4, -1))
    below_a, above_b, ready = lax.optimization_barrier((below_a, above_b, ready))
    below_a, above_b = pl.pallas_call(
        stay_kernel,
        out_shape=(jax.ShapeDtypeStruct(below_a.shape, BF16),) * 2,
        in_specs=[ANY] * 2,
        out_specs=(ANY,) * 2,
        input_output_aliases={0: 0, 1: 1},
        compiler_params=PARAMS,
        cost_estimate=pl.CostEstimate(flops=1 << 30, bytes_accessed=1 << 20, transcendentals=0),
        name="stay",
    )(below_a, above_b)
    far_a = lax.ppermute(below_a, Y, turn(4, 1))
    far_b = lax.ppermute(above_b, Y, turn(4, -1))
    across, below_b, above_a = lax.optimization_barrier((across, below_b, above_a))
    below_x = lax.ppermute(across, Y, turn(4, 1))
    above_x = lax.ppermute(across, Y, turn(4, -1))
    far_xa = lax.ppermute(far_a, "xh", flip(2, 1))
    far_xb = lax.ppermute(far_b, "xh", flip(2, 1))
    return (own, across, below_a, below_b, above_a, above_b), (below_x, above_x, far_a, far_b, far_xa, far_xb), ready


def stay_kernel(*refs):
    pass


def split_kernel(whole, early, late, sems):
    half = early.shape[0]
    first = pltpu.make_async_copy(whole.at[pl.ds(0, half), :], early, sems.at[0])
    second = pltpu.make_async_copy(whole.at[pl.ds(half, half), :], late, sems.at[1])
    first.start()
    second.start()
    first.wait()
    second.wait()


def place_on_y():
    return lax.axis_index("yh") * 2 + lax.axis_index("yl")


def prepare_kernel(lags, factor, library, anchors, spread, lnorm, picks, scale, for_up, for_down):
    rows, width = library.shape
    wide = picks.shape[0]
    squares = jnp.zeros((rows, 128), F32)
    for c in range(0, width, 128):
        part = library[:, c : c + 128].astype(F32)
        squares = squares + part * part
    squares = jnp.concatenate([squares, jnp.zeros((wide - rows, 128), F32)], axis=0)
    norm = jnp.sum(squares.T, axis=0, keepdims=True)
    norm = jnp.broadcast_to(norm, lnorm.shape)
    total = norm
    for lag in range(1, lags):
        total = total + pltpu.roll(norm, lag, 1)
    lnorm[...] = total
    spots = lax.broadcasted_iota(jnp.int32, picks.shape, 0)
    picks[...] = jnp.where(spots == anchors[...], 1.0, 0.0).astype(BF16)
    count = scale.shape[0]
    wider = jnp.concatenate([spread[...] * factor, jnp.ones((1, 128 - count), F32)], axis=1)
    scale[...] = jnp.broadcast_to(wider, (128, 128)).T[:count, :]
    quarter = for_up.shape[1]
    odd = lax.axis_index("yl")
    for_up[...] = library[:, pl.ds(pl.multiple_of((1 + 2 * odd) * quarter, quarter), quarter)]
    for_down[...] = library[:, pl.ds(pl.multiple_of((2 - 2 * odd) * quarter, quarter), quarter)]


def cross_rows(lags, pieces, block, lnorm, acc):
    rows, width = block.shape
    acc[...] = jnp.zeros_like(acc)
    lhs = jnp.concatenate([p[...] for p in pieces], axis=0)
    acc[:, :rows] = lax.dot_general(lhs, block[...], (((1,), (1,)), ((), ())), preferred_element_type=F32)
    norms = jnp.zeros((acc.shape[0], 128), F32)
    for c in range(0, width, 128):
        part = lhs[:, c : c + 128].astype(F32)
        norms = norms + part * part
    norms = jnp.sum(norms, axis=1, keepdims=True)
    count = acc.shape[0] // 4 // lags
    values = []
    for r in range(4):
        cross = jnp.zeros((count, acc.shape[1]), F32)
        tnorm = jnp.zeros((count, 1), F32)
        for lag in range(lags):
            at = (r * lags + lag) * count
            here = acc[at : at + count, :]
            cross = cross + (pltpu.roll(here, lag, 1) if lag else here)
            tnorm = tnorm + norms[at : at + count]
        values.append(tnorm + lnorm[:1, :] - 2.0 * cross)
    return values


def at_anchors(value, picks):
    first = value.astype(BF16)
    rest = value - first.astype(F32)
    second = rest.astype(BF16)
    third = (rest - second.astype(F32)).astype(BF16)
    parts = jnp.concatenate([first, second, third], axis=0)
    parts = jnp.dot(parts, picks[...], preferred_element_type=F32)
    n = value.shape[0]
    return parts[:n] + parts[n : 2 * n] + parts[2 * n :]


def near_kernel(lags, *refs):
    pieces, (block, lnorm, picks, out, acc) = refs[:6], refs[6:]
    values = cross_rows(lags, pieces, block, lnorm, acc)
    out[...] = at_anchors(jnp.concatenate(values, axis=0), picks)


def away_kernel(lags, *refs):
    pieces, (block, lnorm, picks, near, out, acc) = refs[:6], refs[6:]
    values = cross_rows(lags, pieces, block, lnorm, acc)
    count = values[0].shape[0]
    value = at_anchors(jnp.concatenate(values, axis=0), picks)
    y, xh = place_on_y(), lax.axis_index("xh")
    for r, (dy, dx) in enumerate(NEAR + AWAY):
        owner = lax.rem(y + dy, 4) * 2 + lax.rem(xh + dx, 2)
        source, at = (near, r) if r < 4 else (value, r - 4)
        out[pl.ds(pl.multiple_of(owner * count, count), count), :] = source[at * count : (at + 1) * count, :]


def weights_kernel(rows, dist, scale, picks, out):
    scores = -dist[...] / scale[:, :1]
    top = jnp.max(scores, axis=1, keepdims=True)
    top_hi, top_lo = halves(top)
    weights = jnp.exp(scores - (top_hi + top_lo)).astype(BF16)
    tot_hi, tot_lo = halves(jnp.sum(weights.astype(F32), axis=1, keepdims=True))
    spread_out = lax.dot_general(weights, picks[...], (((1,), (1,)), ((), ())), preferred_element_type=F32)
    lane = lax.broadcasted_iota(jnp.int32, spread_out.shape, 1)
    for at, fact in enumerate((top_hi, top_lo, tot_hi, tot_lo)):
        spread_out = jnp.where(lane == rows + at, fact, spread_out)
    out[...] = spread_out.astype(BF16)


def halves(value):
    first = value.astype(BF16).astype(F32)
    return first, (value - first).astype(BF16).astype(F32)


def in_lanes(columns):
    lane = lax.broadcasted_iota(jnp.int32, (columns[0].shape[0], 128), 1)
    value = columns[-1]
    for i in range(len(columns) - 2, -1, -1):
        value = jnp.where(lane == i, columns[i], value)
    return value


def by_target(shape, count):
    row, col = lax.broadcasted_iota(jnp.int32, shape, 0), lax.broadcasted_iota(jnp.int32, shape, 1)
    targets = shape[0] // count
    return jnp.where(lax.rem(row, count) * targets + lax.div(row, count) == col, 1.0, 0.0).astype(BF16)


def mixing(leads, w, perm, rows):
    wide = w.shape[1]
    count = leads.shape[0]
    weights = w[...].astype(F32)
    stack = jnp.concatenate([pltpu.roll(weights, leads[k], 1) for k in range(count)], axis=0).astype(BF16)
    mixed = jnp.dot(perm, stack, preferred_element_type=F32).astype(BF16)[:, :rows]
    fact = jnp.concatenate([w[:, wide - 128 :]] * count, axis=0)
    return mixed, pltpu.roll(jnp.dot(perm, fact, preferred_element_type=F32), wide - rows, 1)


def compose_own_kernel(leads, own, block, out, facts, order):
    rows = block.shape[0]
    quarter = out.shape[1] // 2
    perm = by_target(order.shape, leads.shape[0])
    order[...] = perm
    mixed, facts[...] = mixing(leads, own, perm, rows)
    odd = lax.axis_index("yl")
    for side, start in enumerate((2 * odd, 3 - 2 * odd)):
        mine = block[:, pl.ds(pl.multiple_of(start * quarter, quarter), quarter)]
        out[:, side * quarter : (side + 1) * quarter] = jnp.dot(mixed, mine, preferred_element_type=F32)


def compose_kernel(leads, partial, own_facts, order, up, down, block_up, block_down, out):
    rows, quarter = block_up.shape
    fact = own_facts[...]
    perm = order[...]
    step = 512
    columns = []
    for side, (w, other) in enumerate(((up, block_up), (down, block_down))):
        mixed, there = mixing(leads, w, perm, rows)
        tops = [f[:, 0:1] + f[:, 1:2] for f in (fact, there)]
        totals = [f[:, 2:3] + f[:, 3:4] for f in (fact, there)]
        larger = tops[0] >= tops[1]
        top = jnp.where(larger, tops[0], tops[1])
        first, second = jnp.exp(tops[0] - top), jnp.exp(tops[1] - top)
        columns += [jnp.where(larger, fact[:, j : j + 1], there[:, j : j + 1]) for j in range(2)]
        columns += halves(first * totals[0] + second * totals[1])
        for c in range(0, quarter, step):
            at = side * quarter + c
            value = second * jnp.dot(mixed, other[:, c : c + step], preferred_element_type=F32)
            out[:, at : at + step] = (value + first * partial[:, at : at + step]).astype(BF16)
    out[:, 2 * quarter :] = in_lanes(columns).astype(BF16)


def combine_kernel(parts, out):
    n, rows, wide = parts.shape
    count, lead_n, width = out.shape
    quarter = width // 4
    facts = [parts[b, :, wide - 128 :].astype(F32) for b in range(n)]
    step = 512
    for q in range(4):
        odd, side = ((0, 0), (1, 1), (1, 0), (0, 1))[q]
        sources = [b for b in range(n) if (b // 2) % 2 == odd]
        at = 4 * side
        tops = [facts[b][:, at : at + 1] + facts[b][:, at + 1 : at + 2] for b in sources]
        top = functools.reduce(jnp.maximum, tops)
        factors = [jnp.exp(t - top) for t in tops]
        total = sum(f * (facts[b][:, at + 2 : at + 3] + facts[b][:, at + 3 : at + 4]) for f, b in zip(factors, sources))
        factors = [f / total for f in factors]
        for c in range(0, quarter, step):
            from_c = side * quarter + c
            summed = sum(f * parts[b, :, from_c : from_c + step].astype(F32) for f, b in zip(factors, sources))
            summed = summed.reshape(count, lead_n, step).astype(BF16)
            out[:, :, q * quarter + c : q * quarter + c + step] = summed


def total_over_space(value, arriving):
    value = value + lax.ppermute(value, "co", flip(2, 1))
    both = [(z * 2 + x, (z ^ 1) * 2 + (x ^ 1)) for z in range(8) for x in range(2)]
    value = (value + lax.ppermute(value, "xl", flip(2, 1))) + (lax.ppermute(value, "z", flip(8, 1)) + lax.ppermute(value, ("z", "xl"), both))
    three = lax.ppermute(value, "z", [(z, (z - 3) % 8 if z % 2 == 0 else (z + 3) % 8) for z in range(8)])
    two = lax.ppermute(value, "z", [(z, (z - 2) % 8 if z % 2 == 0 else (z + 2) % 8) for z in range(8)])
    last, arriving = lax.optimization_barrier((value, arriving))
    one = lax.ppermute(last, "z", [(z, (z - 1) % 8 if z % 2 == 0 else (z + 1) % 8) for z in range(8)])
    return value + one + two + three, arriving


def per_device(targets, library, anchors, leads, spread):
    lags, count, width = targets.shape
    rows = library.shape[0]
    lead_n = leads.shape[0]
    n_lib = lax.axis_size(LIB)
    n_target = count * n_lib
    wide = -(-rows // 128) * 128
    scale = math.sqrt(lags * width * lax.axis_size(SPACE))
    quarter = width // 4

    n_anchor = anchors.shape[0]
    ready = pl.pallas_call(
        functools.partial(prepare_kernel, lags, scale),
        out_shape=(
            jax.ShapeDtypeStruct((8, wide), F32),
            jax.ShapeDtypeStruct((wide, n_anchor), BF16),
            jax.ShapeDtypeStruct((n_target, 128), F32),
            jax.ShapeDtypeStruct((rows, quarter), BF16),
            jax.ShapeDtypeStruct((rows, quarter), BF16),
        ),
        in_specs=[VM] * 3,
        out_specs=(VM,) * 5,
        compiler_params=PARAMS,
        cost_estimate=pl.CostEstimate(flops=2 * rows * width, bytes_accessed=4 << 20, transcendentals=0),
        name="prepare",
    )(library, anchors.reshape(1, n_anchor), spread.reshape(1, n_target))
    near, away, ready = gather_targets(targets, ready)
    lnorm, picks, scales, for_up, for_down = ready

    flops = lags * n_target * wide * width
    near_dist = pl.pallas_call(
        functools.partial(near_kernel, lags),
        out_shape=jax.ShapeDtypeStruct((n_target // 2, n_anchor), F32),
        in_specs=[VM] * 9,
        out_specs=VM,
        scratch_shapes=[pltpu.VMEM((lags * n_target // 2, wide), F32)],
        compiler_params=PARAMS,
        cost_estimate=pl.CostEstimate(flops=flops, bytes_accessed=5 << 20, transcendentals=0),
        name="near",
    )(*near, library, lnorm, picks)

    for_up, for_down, near_dist = lax.optimization_barrier((for_up, for_down, near_dist))
    block_down = lax.ppermute(for_up, Y, turn(4, 1))
    block_up = lax.ppermute(for_down, Y, turn(4, -1))

    partial_dist = pl.pallas_call(
        functools.partial(away_kernel, lags),
        out_shape=jax.ShapeDtypeStruct((n_target, n_anchor), F32),
        in_specs=[VM] * 10,
        out_specs=VM,
        scratch_shapes=[pltpu.VMEM((lags * n_target // 2, wide), F32)],
        compiler_params=PARAMS,
        cost_estimate=pl.CostEstimate(flops=flops, bytes_accessed=5 << 20, transcendentals=0),
        name="away",
    )(*away, library, lnorm, picks, near_dist)

    dist, (block_up, block_down) = total_over_space(partial_dist, (block_up, block_down))
    own = pl.pallas_call(
        functools.partial(weights_kernel, rows),
        out_shape=jax.ShapeDtypeStruct((n_target, wide), BF16),
        in_specs=[VM] * 3,
        out_specs=VM,
        compiler_params=PARAMS,
        cost_estimate=pl.CostEstimate(flops=2 * n_target * wide * 256, bytes_accessed=1 << 20, transcendentals=n_target * 256),
        name="weights",
    )(dist, scales, picks)
    down = lax.ppermute(own, Y, turn(4, 1))
    up = lax.ppermute(own, Y, turn(4, -1))

    partial, facts, order = pl.pallas_call(
        compose_own_kernel,
        out_shape=(
            jax.ShapeDtypeStruct((lead_n * n_target, 2 * quarter), F32),
            jax.ShapeDtypeStruct((lead_n * n_target, 128), F32),
            jax.ShapeDtypeStruct((lead_n * n_target, lead_n * n_target), BF16),
        ),
        in_specs=[SM] + [VM] * 2,
        out_specs=(VM,) * 3,
        compiler_params=PARAMS,
        cost_estimate=pl.CostEstimate(flops=lead_n * n_target * rows * width, bytes_accessed=5 << 20, transcendentals=0),
        name="compose_own",
    )(leads, own, library)
    parts = pl.pallas_call(
        compose_kernel,
        out_shape=jax.ShapeDtypeStruct((lead_n * n_target, 2 * quarter + 128), BF16),
        in_specs=[SM] + [VM] * 7,
        out_specs=VM,
        compiler_params=PARAMS,
        cost_estimate=pl.CostEstimate(flops=lead_n * n_target * rows * width, bytes_accessed=5 << 20, transcendentals=0),
        name="compose",
    )(leads, partial, facts, order, up, down, block_up, block_down)

    parts = parts.reshape(n_lib, lead_n * count, 2 * quarter + 128)
    parts = lax.all_to_all(parts, LIB, 0, 0, tiled=True)

    return pl.pallas_call(
        combine_kernel,
        out_shape=jax.ShapeDtypeStruct((count, lead_n, width), BF16),
        in_specs=[VM],
        out_specs=VM,
        compiler_params=PARAMS,
        cost_estimate=pl.CostEstimate(flops=2 * n_target * lead_n * width, bytes_accessed=3 << 20, transcendentals=0),
        name="combine",
    )(parts)


def solution(mesh):
    fine = Mesh(mesh.devices.reshape(8, 2, 2, 2, 2, 2), SPACE + LIB)
    placed = (P(None, LIB, SPACE), P(LIB, SPACE), P(LIB), P(), P())
    return jax.shard_map(per_device, mesh=fine, in_specs=placed, out_specs=P(LIB, None, SPACE), check_vma=False)
```

```python
import functools
import math

import jax
import jax.numpy as jnp
from jax import lax
from jax.experimental import pallas as pl
from jax.experimental.pallas import tpu as pltpu
from jax.sharding import Mesh, PartitionSpec as P

F32 = jnp.float32
BF16 = jnp.bfloat16
Y = ("yh", "yl")
LIB = ("yh", "yl", "xh")
SPACE = ("z", "xl", "co")
VM = pl.BlockSpec(memory_space=pltpu.VMEM)
SM = pl.BlockSpec(memory_space=pltpu.SMEM)
HB = pl.BlockSpec(memory_space=pltpu.HBM)
PARAMS = pltpu.CompilerParams(vmem_limit_bytes=16 * 1024 * 1024)
NEAR = ((0, 0), (0, 1), (3, 0), (1, 0))
AWAY = ((3, 1), (1, 1), (2, 0), (2, 1))


def flip(n, bit):
    return [(i, i ^ bit) for i in range(n)]


def turn(n, by):
    return [(i, (i + by) % n) for i in range(n)]


def gather_targets(targets, ready):
    lags, count, width = targets.shape
    own = targets.reshape(lags * count, width)
    half = lags * count // 2
    early, late = pl.pallas_call(
        split_kernel,
        out_shape=(jax.ShapeDtypeStruct((half, width), BF16),) * 2,
        in_specs=[HB],
        out_specs=(VM,) * 2,
        scratch_shapes=[pltpu.SemaphoreType.DMA((2,))],
        compiler_params=PARAMS,
        name="split",
    )(own)
    below_a = lax.ppermute(early, Y, turn(4, 1))
    above_b = lax.ppermute(late, Y, turn(4, -1))
    sent, early, late = lax.optimization_barrier((own, early, late))
    across = lax.ppermute(sent, "xh", flip(2, 1))
    below_b = lax.ppermute(late, Y, turn(4, 1))
    above_a = lax.ppermute(early, Y, turn(4, -1))
    below_a, above_b, ready = lax.optimization_barrier((below_a, above_b, ready))
    far_a = lax.ppermute(below_a, Y, turn(4, 1))
    far_b = lax.ppermute(above_b, Y, turn(4, -1))
    across, below_b, above_a = lax.optimization_barrier((across, below_b, above_a))
    below_x = lax.ppermute(across, Y, turn(4, 1))
    above_x = lax.ppermute(across, Y, turn(4, -1))
    far_xa = lax.ppermute(far_a, "xh", flip(2, 1))
    far_xb = lax.ppermute(far_b, "xh", flip(2, 1))
    return (own, across, below_a, below_b, above_a, above_b), (below_x, above_x, far_a, far_b, far_xa, far_xb), ready


def split_kernel(whole, early, late, sems):
    half = early.shape[0]
    first = pltpu.make_async_copy(whole.at[pl.ds(0, half), :], early, sems.at[0])
    second = pltpu.make_async_copy(whole.at[pl.ds(half, half), :], late, sems.at[1])
    first.start()
    second.start()
    first.wait()
    second.wait()


def place_on_y():
    return lax.axis_index("yh") * 2 + lax.axis_index("yl")


def prepare_kernel(lags, factor, library, anchors, spread, lnorm, picks, scale, for_up, for_down):
    rows, width = library.shape
    wide = picks.shape[0]
    squares = jnp.zeros((rows, 128), F32)
    for c in range(0, width, 128):
        part = library[:, c : c + 128].astype(F32)
        squares = squares + part * part
    squares = jnp.concatenate([squares, jnp.zeros((wide - rows, 128), F32)], axis=0)
    norm = jnp.sum(squares.T, axis=0, keepdims=True)
    norm = jnp.broadcast_to(norm, lnorm.shape)
    total = norm
    for lag in range(1, lags):
        total = total + pltpu.roll(norm, lag, 1)
    lnorm[...] = total
    spots = lax.broadcasted_iota(jnp.int32, picks.shape, 0)
    picks[...] = jnp.where(spots == anchors[...], 1.0, 0.0).astype(BF16)
    count = scale.shape[0]
    wider = jnp.concatenate([spread[...] * factor, jnp.ones((1, 128 - count), F32)], axis=1)
    scale[...] = jnp.broadcast_to(wider, (128, 128)).T[:count, :]
    quarter = for_up.shape[1]
    odd = lax.axis_index("yl")
    for_up[...] = library[:, pl.ds(pl.multiple_of((1 + 2 * odd) * quarter, quarter), quarter)]
    for_down[...] = library[:, pl.ds(pl.multiple_of((2 - 2 * odd) * quarter, quarter), quarter)]


def cross_rows(lags, pieces, block, lnorm, acc):
    rows, width = block.shape
    acc[...] = jnp.zeros_like(acc)
    lhs = jnp.concatenate([p[...] for p in pieces], axis=0)
    acc[:, :rows] = lax.dot_general(lhs, block[...], (((1,), (1,)), ((), ())), preferred_element_type=F32)
    norms = jnp.zeros((acc.shape[0], 128), F32)
    for c in range(0, width, 128):
        part = lhs[:, c : c + 128].astype(F32)
        norms = norms + part * part
    norms = jnp.sum(norms, axis=1, keepdims=True)
    count = acc.shape[0] // 4 // lags
    values = []
    for r in range(4):
        cross = jnp.zeros((count, acc.shape[1]), F32)
        tnorm = jnp.zeros((count, 1), F32)
        for lag in range(lags):
            at = (r * lags + lag) * count
            here = acc[at : at + count, :]
            cross = cross + (pltpu.roll(here, lag, 1) if lag else here)
            tnorm = tnorm + norms[at : at + count]
        values.append(tnorm + lnorm[:1, :] - 2.0 * cross)
    return values


def at_anchors(value, picks):
    first = value.astype(BF16)
    rest = value - first.astype(F32)
    second = rest.astype(BF16)
    third = (rest - second.astype(F32)).astype(BF16)
    parts = jnp.concatenate([first, second, third], axis=0)
    parts = jnp.dot(parts, picks[...], preferred_element_type=F32)
    n = value.shape[0]
    return parts[:n] + parts[n : 2 * n] + parts[2 * n :]


def near_kernel(lags, *refs):
    pieces, (block, lnorm, picks, out, acc) = refs[:6], refs[6:]
    values = cross_rows(lags, pieces, block, lnorm, acc)
    out[...] = at_anchors(jnp.concatenate(values, axis=0), picks)


def away_kernel(lags, *refs):
    pieces, (block, lnorm, picks, near, out, acc) = refs[:6], refs[6:]
    values = cross_rows(lags, pieces, block, lnorm, acc)
    count = values[0].shape[0]
    value = at_anchors(jnp.concatenate(values, axis=0), picks)
    y, xh = place_on_y(), lax.axis_index("xh")
    for r, (dy, dx) in enumerate(NEAR + AWAY):
        owner = lax.rem(y + dy, 4) * 2 + lax.rem(xh + dx, 2)
        source, at = (near, r) if r < 4 else (value, r - 4)
        out[pl.ds(pl.multiple_of(owner * count, count), count), :] = source[at * count : (at + 1) * count, :]


def weights_kernel(rows, dist, scale, picks, out):
    scores = -dist[...] / scale[:, :1]
    top = jnp.max(scores, axis=1, keepdims=True)
    top_hi, top_lo = halves(top)
    weights = jnp.exp(scores - (top_hi + top_lo)).astype(BF16)
    tot_hi, tot_lo = halves(jnp.sum(weights.astype(F32), axis=1, keepdims=True))
    spread_out = lax.dot_general(weights, picks[...], (((1,), (1,)), ((), ())), preferred_element_type=F32)
    lane = lax.broadcasted_iota(jnp.int32, spread_out.shape, 1)
    for at, fact in enumerate((top_hi, top_lo, tot_hi, tot_lo)):
        spread_out = jnp.where(lane == rows + at, fact, spread_out)
    out[...] = spread_out.astype(BF16)


def halves(value):
    first = value.astype(BF16).astype(F32)
    return first, (value - first).astype(BF16).astype(F32)


def in_lanes(columns):
    lane = lax.broadcasted_iota(jnp.int32, (columns[0].shape[0], 128), 1)
    value = columns[-1]
    for i in range(len(columns) - 2, -1, -1):
        value = jnp.where(lane == i, columns[i], value)
    return value


def by_target(shape, count):
    row, col = lax.broadcasted_iota(jnp.int32, shape, 0), lax.broadcasted_iota(jnp.int32, shape, 1)
    targets = shape[0] // count
    return jnp.where(lax.rem(row, count) * targets + lax.div(row, count) == col, 1.0, 0.0).astype(BF16)


def mixing(leads, w, perm, rows):
    wide = w.shape[1]
    count = leads.shape[0]
    weights = w[...].astype(F32)
    stack = jnp.concatenate([pltpu.roll(weights, leads[k], 1) for k in range(count)], axis=0).astype(BF16)
    mixed = jnp.dot(perm, stack, preferred_element_type=F32).astype(BF16)[:, :rows]
    fact = jnp.concatenate([w[:, wide - 128 :]] * count, axis=0)
    return mixed, pltpu.roll(jnp.dot(perm, fact, preferred_element_type=F32), wide - rows, 1)


def compose_own_kernel(leads, own, block, out, facts, order):
    rows = block.shape[0]
    quarter = out.shape[1] // 2
    perm = by_target(order.shape, leads.shape[0])
    order[...] = perm
    mixed, facts[...] = mixing(leads, own, perm, rows)
    odd = lax.axis_index("yl")
    for side, start in enumerate((2 * odd, 3 - 2 * odd)):
        mine = block[:, pl.ds(pl.multiple_of(start * quarter, quarter), quarter)]
        out[:, side * quarter : (side + 1) * quarter] = jnp.dot(mixed, mine, preferred_element_type=F32)


def compose_kernel(leads, partial, own_facts, order, up, down, block_up, block_down, out):
    rows, quarter = block_up.shape
    fact = own_facts[...]
    perm = order[...]
    step = 512
    columns = []
    for side, (w, other) in enumerate(((up, block_up), (down, block_down))):
        mixed, there = mixing(leads, w, perm, rows)
        tops = [f[:, 0:1] + f[:, 1:2] for f in (fact, there)]
        totals = [f[:, 2:3] + f[:, 3:4] for f in (fact, there)]
        larger = tops[0] >= tops[1]
        top = jnp.where(larger, tops[0], tops[1])
        first, second = jnp.exp(tops[0] - top), jnp.exp(tops[1] - top)
        columns += [jnp.where(larger, fact[:, j : j + 1], there[:, j : j + 1]) for j in range(2)]
        columns += halves(first * totals[0] + second * totals[1])
        for c in range(0, quarter, step):
            at = side * quarter + c
            value = second * jnp.dot(mixed, other[:, c : c + step], preferred_element_type=F32)
            out[:, at : at + step] = (value + first * partial[:, at : at + step]).astype(BF16)
    out[:, 2 * quarter :] = in_lanes(columns).astype(BF16)


def combine_kernel(parts, out):
    n, rows, wide = parts.shape
    count, lead_n, width = out.shape
    quarter = width // 4
    facts = [parts[b, :, wide - 128 :].astype(F32) for b in range(n)]
    step = 512
    for q in range(4):
        odd, side = ((0, 0), (1, 1), (1, 0), (0, 1))[q]
        sources = [b for b in range(n) if (b // 2) % 2 == odd]
        at = 4 * side
        tops = [facts[b][:, at : at + 1] + facts[b][:, at + 1 : at + 2] for b in sources]
        top = functools.reduce(jnp.maximum, tops)
        factors = [jnp.exp(t - top) for t in tops]
        total = sum(f * (facts[b][:, at + 2 : at + 3] + facts[b][:, at + 3 : at + 4]) for f, b in zip(factors, sources))
        factors = [f / total for f in factors]
        for c in range(0, quarter, step):
            from_c = side * quarter + c
            summed = sum(f * parts[b, :, from_c : from_c + step].astype(F32) for f, b in zip(factors, sources))
            summed = summed.reshape(count, lead_n, step).astype(BF16)
            out[:, :, q * quarter + c : q * quarter + c + step] = summed


def total_over_space(value, arriving):
    value = value + lax.ppermute(value, "co", flip(2, 1))
    both = [(z * 2 + x, (z ^ 1) * 2 + (x ^ 1)) for z in range(8) for x in range(2)]
    value = (value + lax.ppermute(value, "xl", flip(2, 1))) + (lax.ppermute(value, "z", flip(8, 1)) + lax.ppermute(value, ("z", "xl"), both))
    three = lax.ppermute(value, "z", [(z, (z - 3) % 8 if z % 2 == 0 else (z + 3) % 8) for z in range(8)])
    two = lax.ppermute(value, "z", [(z, (z - 2) % 8 if z % 2 == 0 else (z + 2) % 8) for z in range(8)])
    last, arriving = lax.optimization_barrier((value, arriving))
    one = lax.ppermute(last, "z", [(z, (z - 1) % 8 if z % 2 == 0 else (z + 1) % 8) for z in range(8)])
    return value + one + two + three, arriving


def per_device(targets, library, anchors, leads, spread):
    lags, count, width = targets.shape
    rows = library.shape[0]
    lead_n = leads.shape[0]
    n_lib = lax.axis_size(LIB)
    n_target = count * n_lib
    wide = -(-rows // 128) * 128
    scale = math.sqrt(lags * width * lax.axis_size(SPACE))
    quarter = width // 4

    n_anchor = anchors.shape[0]
    ready = pl.pallas_call(
        functools.partial(prepare_kernel, lags, scale),
        out_shape=(
            jax.ShapeDtypeStruct((8, wide), F32),
            jax.ShapeDtypeStruct((wide, n_anchor), BF16),
            jax.ShapeDtypeStruct((n_target, 128), F32),
            jax.ShapeDtypeStruct((rows, quarter), BF16),
            jax.ShapeDtypeStruct((rows, quarter), BF16),
        ),
        in_specs=[VM] * 3,
        out_specs=(VM,) * 5,
        compiler_params=PARAMS,
        cost_estimate=pl.CostEstimate(flops=2 * rows * width, bytes_accessed=4 << 20, transcendentals=0),
        name="prepare",
    )(library, anchors.reshape(1, n_anchor), spread.reshape(1, n_target))
    near, away, ready = gather_targets(targets, ready)
    lnorm, picks, scales, for_up, for_down = ready

    flops = lags * n_target * wide * width
    near_dist = pl.pallas_call(
        functools.partial(near_kernel, lags),
        out_shape=jax.ShapeDtypeStruct((n_target // 2, n_anchor), F32),
        in_specs=[VM] * 9,
        out_specs=VM,
        scratch_shapes=[pltpu.VMEM((lags * n_target // 2, wide), F32)],
        compiler_params=PARAMS,
        cost_estimate=pl.CostEstimate(flops=flops, bytes_accessed=5 << 20, transcendentals=0),
        name="near",
    )(*near, library, lnorm, picks)

    for_up, for_down, near_dist = lax.optimization_barrier((for_up, for_down, near_dist))
    block_down = lax.ppermute(for_up, Y, turn(4, 1))
    block_up = lax.ppermute(for_down, Y, turn(4, -1))

    partial_dist = pl.pallas_call(
        functools.partial(away_kernel, lags),
        out_shape=jax.ShapeDtypeStruct((n_target, n_anchor), F32),
        in_specs=[VM] * 10,
        out_specs=VM,
        scratch_shapes=[pltpu.VMEM((lags * n_target // 2, wide), F32)],
        compiler_params=PARAMS,
        cost_estimate=pl.CostEstimate(flops=flops, bytes_accessed=5 << 20, transcendentals=0),
        name="away",
    )(*away, library, lnorm, picks, near_dist)

    dist, (block_up, block_down) = total_over_space(partial_dist, (block_up, block_down))
    own = pl.pallas_call(
        functools.partial(weights_kernel, rows),
        out_shape=jax.ShapeDtypeStruct((n_target, wide), BF16),
        in_specs=[VM] * 3,
        out_specs=VM,
        compiler_params=PARAMS,
        cost_estimate=pl.CostEstimate(flops=2 * n_target * wide * 256, bytes_accessed=1 << 20, transcendentals=n_target * 256),
        name="weights",
    )(dist, scales, picks)
    down = lax.ppermute(own, Y, turn(4, 1))
    up = lax.ppermute(own, Y, turn(4, -1))

    partial, facts, order = pl.pallas_call(
        compose_own_kernel,
        out_shape=(
            jax.ShapeDtypeStruct((lead_n * n_target, 2 * quarter), F32),
            jax.ShapeDtypeStruct((lead_n * n_target, 128), F32),
            jax.ShapeDtypeStruct((lead_n * n_target, lead_n * n_target), BF16),
        ),
        in_specs=[SM] + [VM] * 2,
        out_specs=(VM,) * 3,
        compiler_params=PARAMS,
        cost_estimate=pl.CostEstimate(flops=lead_n * n_target * rows * width, bytes_accessed=5 << 20, transcendentals=0),
        name="compose_own",
    )(leads, own, library)
    parts = pl.pallas_call(
        compose_kernel,
        out_shape=jax.ShapeDtypeStruct((lead_n * n_target, 2 * quarter + 128), BF16),
        in_specs=[SM] + [VM] * 7,
        out_specs=VM,
        compiler_params=PARAMS,
        cost_estimate=pl.CostEstimate(flops=lead_n * n_target * rows * width, bytes_accessed=5 << 20, transcendentals=0),
        name="compose",
    )(leads, partial, facts, order, up, down, block_up, block_down)

    parts = parts.reshape(n_lib, lead_n * count, 2 * quarter + 128)
    parts = lax.all_to_all(parts, LIB, 0, 0, tiled=True)

    return pl.pallas_call(
        combine_kernel,
        out_shape=jax.ShapeDtypeStruct((count, lead_n, width), BF16),
        in_specs=[VM],
        out_specs=VM,
        compiler_params=PARAMS,
        cost_estimate=pl.CostEstimate(flops=2 * n_target * lead_n * width, bytes_accessed=3 << 20, transcendentals=0),
        name="combine",
    )(parts)


def solution(mesh):
    fine = Mesh(mesh.devices.reshape(8, 2, 2, 2, 2, 2), SPACE + LIB)
    placed = (P(None, LIB, SPACE), P(LIB, SPACE), P(LIB), P(), P())
    return jax.shard_map(per_device, mesh=fine, in_specs=placed, out_specs=P(LIB, None, SPACE), check_vma=False)
```

```python
import functools
import math

import jax
import jax.numpy as jnp
from jax import lax
from jax.experimental import pallas as pl
from jax.experimental.pallas import tpu as pltpu
from jax.sharding import Mesh, PartitionSpec as P

F32 = jnp.float32
BF16 = jnp.bfloat16
Y = ("yh", "yl")
LIB = ("yh", "yl", "xh")
SPACE = ("z", "xl", "co")
VM = pl.BlockSpec(memory_space=pltpu.VMEM)
SM = pl.BlockSpec(memory_space=pltpu.SMEM)
HB = pl.BlockSpec(memory_space=pltpu.HBM)
PARAMS = pltpu.CompilerParams(vmem_limit_bytes=16 * 1024 * 1024)
NEAR = ((0, 0), (0, 1), (3, 0), (1, 0))
AWAY = ((3, 1), (1, 1), (2, 0), (2, 1))


def flip(n, bit):
    return [(i, i ^ bit) for i in range(n)]


def turn(n, by):
    return [(i, (i + by) % n) for i in range(n)]


def gather_targets(targets, ready):
    lags, count, width = targets.shape
    own = targets.reshape(lags * count, width)
    half = lags * count // 2
    early, late = pl.pallas_call(
        split_kernel,
        out_shape=(jax.ShapeDtypeStruct((half, width), BF16),) * 2,
        in_specs=[HB],
        out_specs=(VM,) * 2,
        scratch_shapes=[pltpu.SemaphoreType.DMA((2,))],
        compiler_params=PARAMS,
        name="split",
    )(own)
    below_a = lax.ppermute(early, Y, turn(4, 1))
    above_b = lax.ppermute(late, Y, turn(4, -1))
    sent, early, late = lax.optimization_barrier((own, early, late))
    across = lax.ppermute(sent, "xh", flip(2, 1))
    below_b = lax.ppermute(late, Y, turn(4, 1))
    above_a = lax.ppermute(early, Y, turn(4, -1))
    far_a = lax.ppermute(below_a, Y, turn(4, 1))
    far_b = lax.ppermute(above_b, Y, turn(4, -1))
    across, below_b, above_a, ready = lax.optimization_barrier((across, below_b, above_a, ready))
    below_x = lax.ppermute(across, Y, turn(4, 1))
    above_x = lax.ppermute(across, Y, turn(4, -1))
    far_xa = lax.ppermute(far_a, "xh", flip(2, 1))
    far_xb = lax.ppermute(far_b, "xh", flip(2, 1))
    return (own, across, below_a, below_b, above_a, above_b), (below_x, above_x, far_a, far_b, far_xa, far_xb), ready


def split_kernel(whole, early, late, sems):
    half = early.shape[0]
    first = pltpu.make_async_copy(whole.at[pl.ds(0, half), :], early, sems.at[0])
    second = pltpu.make_async_copy(whole.at[pl.ds(half, half), :], late, sems.at[1])
    first.start()
    second.start()
    first.wait()
    second.wait()


def place_on_y():
    return lax.axis_index("yh") * 2 + lax.axis_index("yl")


def prepare_kernel(lags, factor, library, anchors, spread, lnorm, picks, scale, for_up, for_down):
    rows, width = library.shape
    wide = picks.shape[0]
    squares = jnp.zeros((rows, 128), F32)
    for c in range(0, width, 128):
        part = library[:, c : c + 128].astype(F32)
        squares = squares + part * part
    squares = jnp.concatenate([squares, jnp.zeros((wide - rows, 128), F32)], axis=0)
    norm = jnp.sum(squares.T, axis=0, keepdims=True)
    norm = jnp.broadcast_to(norm, lnorm.shape)
    total = norm
    for lag in range(1, lags):
        total = total + pltpu.roll(norm, lag, 1)
    lnorm[...] = total
    spots = lax.broadcasted_iota(jnp.int32, picks.shape, 0)
    picks[...] = jnp.where(spots == anchors[...], 1.0, 0.0).astype(BF16)
    count = scale.shape[0]
    wider = jnp.concatenate([spread[...] * factor, jnp.ones((1, 128 - count), F32)], axis=1)
    scale[...] = jnp.broadcast_to(wider, (128, 128)).T[:count, :]
    quarter = for_up.shape[1]
    odd = lax.axis_index("yl")
    for_up[...] = library[:, pl.ds(pl.multiple_of((1 + 2 * odd) * quarter, quarter), quarter)]
    for_down[...] = library[:, pl.ds(pl.multiple_of((2 - 2 * odd) * quarter, quarter), quarter)]


def cross_rows(lags, pieces, block, lnorm, acc):
    rows, width = block.shape
    acc[...] = jnp.zeros_like(acc)
    lhs = jnp.concatenate([p[...] for p in pieces], axis=0)
    acc[:, :rows] = lax.dot_general(lhs, block[...], (((1,), (1,)), ((), ())), preferred_element_type=F32)
    norms = jnp.zeros((acc.shape[0], 128), F32)
    for c in range(0, width, 128):
        part = lhs[:, c : c + 128].astype(F32)
        norms = norms + part * part
    norms = jnp.sum(norms, axis=1, keepdims=True)
    count = acc.shape[0] // 4 // lags
    values = []
    for r in range(4):
        cross = jnp.zeros((count, acc.shape[1]), F32)
        tnorm = jnp.zeros((count, 1), F32)
        for lag in range(lags):
            at = (r * lags + lag) * count
            here = acc[at : at + count, :]
            cross = cross + (pltpu.roll(here, lag, 1) if lag else here)
            tnorm = tnorm + norms[at : at + count]
        values.append(tnorm + lnorm[:1, :] - 2.0 * cross)
    return values


def at_anchors(value, picks):
    first = value.astype(BF16)
    rest = value - first.astype(F32)
    second = rest.astype(BF16)
    third = (rest - second.astype(F32)).astype(BF16)
    parts = jnp.concatenate([first, second, third], axis=0)
    parts = jnp.dot(parts, picks[...], preferred_element_type=F32)
    n = value.shape[0]
    return parts[:n] + parts[n : 2 * n] + parts[2 * n :]


def near_kernel(lags, *refs):
    pieces, (block, lnorm, picks, out, acc) = refs[:6], refs[6:]
    values = cross_rows(lags, pieces, block, lnorm, acc)
    out[...] = at_anchors(jnp.concatenate(values, axis=0), picks)


def away_kernel(lags, *refs):
    pieces, (block, lnorm, picks, near, out, acc) = refs[:6], refs[6:]
    values = cross_rows(lags, pieces, block, lnorm, acc)
    count = values[0].shape[0]
    value = at_anchors(jnp.concatenate(values, axis=0), picks)
    y, xh = place_on_y(), lax.axis_index("xh")
    for r, (dy, dx) in enumerate(NEAR + AWAY):
        owner = lax.rem(y + dy, 4) * 2 + lax.rem(xh + dx, 2)
        source, at = (near, r) if r < 4 else (value, r - 4)
        out[pl.ds(pl.multiple_of(owner * count, count), count), :] = source[at * count : (at + 1) * count, :]


def weights_kernel(rows, dist, scale, picks, out):
    scores = -dist[...] / scale[:, :1]
    top = jnp.max(scores, axis=1, keepdims=True)
    top_hi, top_lo = halves(top)
    weights = jnp.exp(scores - (top_hi + top_lo)).astype(BF16)
    tot_hi, tot_lo = halves(jnp.sum(weights.astype(F32), axis=1, keepdims=True))
    spread_out = lax.dot_general(weights, picks[...], (((1,), (1,)), ((), ())), preferred_element_type=F32)
    lane = lax.broadcasted_iota(jnp.int32, spread_out.shape, 1)
    for at, fact in enumerate((top_hi, top_lo, tot_hi, tot_lo)):
        spread_out = jnp.where(lane == rows + at, fact, spread_out)
    out[...] = spread_out.astype(BF16)


def halves(value):
    first = value.astype(BF16).astype(F32)
    return first, (value - first).astype(BF16).astype(F32)


def in_lanes(columns):
    lane = lax.broadcasted_iota(jnp.int32, (columns[0].shape[0], 128), 1)
    value = columns[-1]
    for i in range(len(columns) - 2, -1, -1):
        value = jnp.where(lane == i, columns[i], value)
    return value


def by_target(shape, count):
    row, col = lax.broadcasted_iota(jnp.int32, shape, 0), lax.broadcasted_iota(jnp.int32, shape, 1)
    targets = shape[0] // count
    return jnp.where(lax.rem(row, count) * targets + lax.div(row, count) == col, 1.0, 0.0).astype(BF16)


def mixing(leads, w, perm, rows):
    wide = w.shape[1]
    count = leads.shape[0]
    weights = w[...].astype(F32)
    stack = jnp.concatenate([pltpu.roll(weights, leads[k], 1) for k in range(count)], axis=0).astype(BF16)
    mixed = jnp.dot(perm, stack, preferred_element_type=F32).astype(BF16)[:, :rows]
    fact = jnp.concatenate([w[:, wide - 128 :]] * count, axis=0)
    return mixed, pltpu.roll(jnp.dot(perm, fact, preferred_element_type=F32), wide - rows, 1)


def compose_own_kernel(leads, own, block, out, facts, order):
    rows = block.shape[0]
    quarter = out.shape[1] // 2
    perm = by_target(order.shape, leads.shape[0])
    order[...] = perm
    mixed, facts[...] = mixing(leads, own, perm, rows)
    odd = lax.axis_index("yl")
    for side, start in enumerate((2 * odd, 3 - 2 * odd)):
        mine = block[:, pl.ds(pl.multiple_of(start * quarter, quarter), quarter)]
        out[:, side * quarter : (side + 1) * quarter] = jnp.dot(mixed, mine, preferred_element_type=F32)


def compose_kernel(leads, partial, own_facts, order, up, down, block_up, block_down, out):
    rows, quarter = block_up.shape
    fact = own_facts[...]
    perm = order[...]
    step = 512
    columns = []
    for side, (w, other) in enumerate(((up, block_up), (down, block_down))):
        mixed, there = mixing(leads, w, perm, rows)
        tops = [f[:, 0:1] + f[:, 1:2] for f in (fact, there)]
        totals = [f[:, 2:3] + f[:, 3:4] for f in (fact, there)]
        larger = tops[0] >= tops[1]
        top = jnp.where(larger, tops[0], tops[1])
        first, second = jnp.exp(tops[0] - top), jnp.exp(tops[1] - top)
        columns += [jnp.where(larger, fact[:, j : j + 1], there[:, j : j + 1]) for j in range(2)]
        columns += halves(first * totals[0] + second * totals[1])
        for c in range(0, quarter, step):
            at = side * quarter + c
            value = second * jnp.dot(mixed, other[:, c : c + step], preferred_element_type=F32)
            out[:, at : at + step] = (value + first * partial[:, at : at + step]).astype(BF16)
    out[:, 2 * quarter :] = in_lanes(columns).astype(BF16)


def combine_kernel(parts, out):
    n, rows, wide = parts.shape
    count, lead_n, width = out.shape
    quarter = width // 4
    facts = [parts[b, :, wide - 128 :].astype(F32) for b in range(n)]
    step = 512
    for q in range(4):
        odd, side = ((0, 0), (1, 1), (1, 0), (0, 1))[q]
        sources = [b for b in range(n) if (b // 2) % 2 == odd]
        at = 4 * side
        tops = [facts[b][:, at : at + 1] + facts[b][:, at + 1 : at + 2] for b in sources]
        top = functools.reduce(jnp.maximum, tops)
        factors = [jnp.exp(t - top) for t in tops]
        total = sum(f * (facts[b][:, at + 2 : at + 3] + facts[b][:, at + 3 : at + 4]) for f, b in zip(factors, sources))
        factors = [f / total for f in factors]
        for c in range(0, quarter, step):
            from_c = side * quarter + c
            summed = sum(f * parts[b, :, from_c : from_c + step].astype(F32) for f, b in zip(factors, sources))
            summed = summed.reshape(count, lead_n, step).astype(BF16)
            out[:, :, q * quarter + c : q * quarter + c + step] = summed


def total_over_space(value, arriving):
    value = value + lax.ppermute(value, "co", flip(2, 1))
    both = [(z * 2 + x, (z ^ 1) * 2 + (x ^ 1)) for z in range(8) for x in range(2)]
    value = (value + lax.ppermute(value, "xl", flip(2, 1))) + (lax.ppermute(value, "z", flip(8, 1)) + lax.ppermute(value, ("z", "xl"), both))
    three = lax.ppermute(value, "z", [(z, (z - 3) % 8 if z % 2 == 0 else (z + 3) % 8) for z in range(8)])
    two = lax.ppermute(value, "z", [(z, (z - 2) % 8 if z % 2 == 0 else (z + 2) % 8) for z in range(8)])
    last, arriving = lax.optimization_barrier((value, arriving))
    one = lax.ppermute(last, "z", [(z, (z - 1) % 8 if z % 2 == 0 else (z + 1) % 8) for z in range(8)])
    return value + one + two + three, arriving


def per_device(targets, library, anchors, leads, spread):
    lags, count, width = targets.shape
    rows = library.shape[0]
    lead_n = leads.shape[0]
    n_lib = lax.axis_size(LIB)
    n_target = count * n_lib
    wide = -(-rows // 128) * 128
    scale = math.sqrt(lags * width * lax.axis_size(SPACE))
    quarter = width // 4

    n_anchor = anchors.shape[0]
    ready = pl.pallas_call(
        functools.partial(prepare_kernel, lags, scale),
        out_shape=(
            jax.ShapeDtypeStruct((8, wide), F32),
            jax.ShapeDtypeStruct((wide, n_anchor), BF16),
            jax.ShapeDtypeStruct((n_target, 128), F32),
            jax.ShapeDtypeStruct((rows, quarter), BF16),
            jax.ShapeDtypeStruct((rows, quarter), BF16),
        ),
        in_specs=[VM] * 3,
        out_specs=(VM,) * 5,
        compiler_params=PARAMS,
        cost_estimate=pl.CostEstimate(flops=2 * rows * width, bytes_accessed=4 << 20, transcendentals=0),
        name="prepare",
    )(library, anchors.reshape(1, n_anchor), spread.reshape(1, n_target))
    near, away, ready = gather_targets(targets, ready)
    lnorm, picks, scales, for_up, for_down = ready

    flops = lags * n_target * wide * width
    near_dist = pl.pallas_call(
        functools.partial(near_kernel, lags),
        out_shape=jax.ShapeDtypeStruct((n_target // 2, n_anchor), F32),
        in_specs=[VM] * 9,
        out_specs=VM,
        scratch_shapes=[pltpu.VMEM((lags * n_target // 2, wide), F32)],
        compiler_params=PARAMS,
        cost_estimate=pl.CostEstimate(flops=flops, bytes_accessed=5 << 20, transcendentals=0),
        name="near",
    )(*near, library, lnorm, picks)

    for_up, for_down, near_dist = lax.optimization_barrier((for_up, for_down, near_dist))
    block_down = lax.ppermute(for_up, Y, turn(4, 1))
    block_up = lax.ppermute(for_down, Y, turn(4, -1))

    partial_dist = pl.pallas_call(
        functools.partial(away_kernel, lags),
        out_shape=jax.ShapeDtypeStruct((n_target, n_anchor), F32),
        in_specs=[VM] * 10,
        out_specs=VM,
        scratch_shapes=[pltpu.VMEM((lags * n_target // 2, wide), F32)],
        compiler_params=PARAMS,
        cost_estimate=pl.CostEstimate(flops=flops, bytes_accessed=5 << 20, transcendentals=0),
        name="away",
    )(*away, library, lnorm, picks, near_dist)

    dist, (block_up, block_down) = total_over_space(partial_dist, (block_up, block_down))
    own = pl.pallas_call(
        functools.partial(weights_kernel, rows),
        out_shape=jax.ShapeDtypeStruct((n_target, wide), BF16),
        in_specs=[VM] * 3,
        out_specs=VM,
        compiler_params=PARAMS,
        cost_estimate=pl.CostEstimate(flops=2 * n_target * wide * 256, bytes_accessed=1 << 20, transcendentals=n_target * 256),
        name="weights",
    )(dist, scales, picks)
    down = lax.ppermute(own, Y, turn(4, 1))
    up = lax.ppermute(own, Y, turn(4, -1))

    partial, facts, order = pl.pallas_call(
        compose_own_kernel,
        out_shape=(
            jax.ShapeDtypeStruct((lead_n * n_target, 2 * quarter), F32),
            jax.ShapeDtypeStruct((lead_n * n_target, 128), F32),
            jax.ShapeDtypeStruct((lead_n * n_target, lead_n * n_target), BF16),
        ),
        in_specs=[SM] + [VM] * 2,
        out_specs=(VM,) * 3,
        compiler_params=PARAMS,
        cost_estimate=pl.CostEstimate(flops=lead_n * n_target * rows * width, bytes_accessed=5 << 20, transcendentals=0),
        name="compose_own",
    )(leads, own, library)
    parts = pl.pallas_call(
        compose_kernel,
        out_shape=jax.ShapeDtypeStruct((lead_n * n_target, 2 * quarter + 128), BF16),
        in_specs=[SM] + [VM] * 7,
        out_specs=VM,
        compiler_params=PARAMS,
        cost_estimate=pl.CostEstimate(flops=lead_n * n_target * rows * width, bytes_accessed=5 << 20, transcendentals=0),
        name="compose",
    )(leads, partial, facts, order, up, down, block_up, block_down)

    parts = parts.reshape(n_lib, lead_n * count, 2 * quarter + 128)
    parts = lax.all_to_all(parts, LIB, 0, 0, tiled=True)

    return pl.pallas_call(
        combine_kernel,
        out_shape=jax.ShapeDtypeStruct((count, lead_n, width), BF16),
        in_specs=[VM],
        out_specs=VM,
        compiler_params=PARAMS,
        cost_estimate=pl.CostEstimate(flops=2 * n_target * lead_n * width, bytes_accessed=3 << 20, transcendentals=0),
        name="combine",
    )(parts)


def solution(mesh):
    fine = Mesh(mesh.devices.reshape(8, 2, 2, 2, 2, 2), SPACE + LIB)
    placed = (P(None, LIB, SPACE), P(LIB, SPACE), P(LIB), P(), P())
    return jax.shard_map(per_device, mesh=fine, in_specs=placed, out_specs=P(LIB, None, SPACE), check_vma=False)
```
